128 devices in a mesh: gx: 4 (over z_hi, core), yz: 32 (over z_lo, y, x).
Axes of the slice: x: 4, y: 4, z: 4 (z_hi: 2, z_lo: 2; z = z_hi * 2 + z_lo), core: 2. Of those that a mesh axis runs over, the one named last changes fastest.
Arguments:
- positions: float32 [3, 4, 32, 512], P(None, 'gx', 'yz'), may hold values from -0.35 to 0.35
- species: int32 [4, 32, 512], P('gx', 'yz'), may hold values from 0 to 7
- neighbors: int32 [4, 32, 512, 48], P('gx', 'yz'), may hold values from 0 to 4607, as said below
- slot_used: int32 [4, 32, 512, 48], P('gx', 'yz'), may hold values from 0 to 1, as said below
- embed_weight: bfloat16 [24, 128], replicated, may hold values from -1.25 to 1.25
- first_weight: bfloat16 [128, 32], replicated, may hold values from -0.5 to 0.5
- env_weight: bfloat16 [2, 128, 32], replicated, may hold values from -0.5 to 0.5
- latent_weight: bfloat16 [2, 224, 128], replicated, may hold values from -0.375 to 0.375
- mix_weight: bfloat16 [1, 3, 32, 32], replicated, may hold values from -1 to 1
- out_weight: bfloat16 [128, 128], replicated, may hold values from -0.5 to 0.5
- out_vector: float32 [128], replicated, may hold values from -0.5 to 0.5
Outputs:
- atom_energy: float32 [4, 32, 512], P('gx', 'yz')
- forces: float32 [3, 4, 32, 512], P(None, 'gx', 'yz')
The draws below stay inside these ranges and needn't reach their ends.
Inputs may be any that keep to these rules, and one draw needn't show every extreme that they name: `neighbors`: entry (g, y, k, s) names the neighbour in slot s of site k of the device at (g, y), as in the first step. A site's neighbours are distinct lattice points other than its own, at most 2 steps from it along each of x, y and z. `slot_used`: atoms fill each device's sites from site 0 upward. In every row of devices along yz (one gx index), a quarter of the devices hold atoms at all 512 sites and the others at 64 to 128 sites, some exactly 128. A slot is used exactly where its site and the named neighbour site both hold atoms.
All inputs are finite; a program needn't handle non-finite values.
Results may differ from the reference program's by a relative error of at most 0.017.
Values sent between devices are 32-bit elements; how exact they have to be, the bound alone decides.
No kernel may reach another device: no remote copies, remote signals or barrier semaphores. Data moves between devices by JAX's collectives and lax.ppermute only.
A program may use at most 128 MiB of HBM per device.

```python
import math
import jax
import jax.numpy as jnp
import numpy as np
from jax import lax

LX = 8
LY = 8
LZ = 8
NB = 48
NRAD = 8
NSPEC = 8
CH = 32
LATENT = 128
LAYERS = 2
A = 512
LIGHT = 128
N_GX = 4
N_YZ = 32


def lattice_pairs(key):
    key = jax.random.fold_in(key, 11)
    centre_total = N_GX * N_YZ * A
    scores = jax.random.randint(key, (centre_total, 124), 0, 1048576) * 128 + jnp.arange(124, dtype=jnp.int32)[None, :]
    _, chosen = lax.top_k(scores, NB)
    chosen = chosen + (chosen >= 62).astype(jnp.int32)
    step_x = chosen // 25 - 2
    step_y = chosen // 5 % 5 - 2
    step_z = chosen % 5 - 2
    centre_site = jnp.arange(centre_total, dtype=jnp.int32) % A
    centre_x = centre_site // (LY * LZ)
    centre_y = centre_site // LZ % LY
    centre_z = centre_site % LZ
    moved_x = centre_x[:, None] + step_x
    moved_y = centre_y[:, None] + step_y
    side_x = (moved_x + LX) // LX
    side_y = (moved_y + LY) // LY
    far_x = moved_x - (side_x - 1) * LX
    far_y = moved_y - (side_y - 1) * LY
    far_z = (centre_z[:, None] + step_z) % LZ
    far_site = (far_x * LY + far_y) * LZ + far_z
    listed = (side_x * 3 + side_y) * A + far_site
    shape = (N_GX, N_YZ, A, NB)
    return (listed.reshape(shape).astype(jnp.int32), side_x.reshape(shape).astype(jnp.int32), side_y.reshape(shape).astype(jnp.int32), far_site.reshape(shape).astype(jnp.int32))


def atom_counts(key):
    key = jax.random.fold_in(key, 23)
    order_key, count_key = jax.random.split(key)
    scores = jax.random.randint(order_key, (N_GX, N_YZ), 0, 1048576) * N_YZ + jnp.arange(N_YZ, dtype=jnp.int32)[None, :]
    device_rank = jnp.argsort(jnp.argsort(scores, axis=1), axis=1)
    light_counts = jax.random.randint(count_key, (N_GX, N_YZ), LIGHT // 2, LIGHT + 1)
    light_counts = jnp.where(device_rank == N_YZ // 4, LIGHT, light_counts)
    return jnp.where(device_rank < N_YZ // 4, A, light_counts).astype(jnp.int32)


def draw_neighbors(key, part):
    listed, side_x, side_y, far_site = lattice_pairs(key)
    return listed


def draw_slot_used(key, part):
    listed, side_x, side_y, far_site = lattice_pairs(key)
    counts = atom_counts(key)
    home_gx = jnp.arange(N_GX, dtype=jnp.int32)[:, None, None, None]
    home_yz = jnp.arange(N_YZ, dtype=jnp.int32)[None, :, None, None]
    far_gx = (home_gx + side_x - 1) % N_GX
    far_yz = (home_yz + side_y - 1) % N_YZ
    far_count = counts[far_gx, far_yz]
    site_ids = jnp.arange(A, dtype=jnp.int32)[None, None, :, None]
    slot_live = (site_ids < counts[:, :, None, None]) & (far_site < far_count)
    return slot_live.astype(jnp.int32)


def touch_ends(values, stream_key, low, top_value):
    longest = values.shape.index(max(values.shape))
    spots = []
    for shift in (0, 1):
        where = [jax.random.randint(jax.random.fold_in(stream_key, axis), (), 0, length) for axis, length in enumerate(values.shape)]
        where[longest] = (where[longest] + shift) % values.shape[longest]
        spots.append(tuple(where))
    return values.at[spots[0]].set(low).at[spots[1]].set(top_value)


def levels(stream_key, shape, cuts, low, high):
    gain = 1.0
    for dim, blocks in cuts:
        draws = jax.random.uniform(jax.random.fold_in(jax.random.fold_in(stream_key, 6), dim), (blocks,), jnp.float32, low / len(cuts), high / len(cuts))
        gain = gain * jnp.repeat(jnp.exp(draws), shape[dim] // blocks).reshape((-1,) + (1,) * (len(shape) - 1 - dim))
    return gain


def centred(own_key, shape, width, reach, kind=jnp.bfloat16):
    values = jax.random.normal(own_key, shape, jnp.float32) * width
    return jnp.minimum(jnp.maximum(values, -reach), reach).astype(kind)


def setup_inputs(seed: int = 0) -> dict:
    seeds = jax.random.split(jax.random.key(seed), 12)
    positions = jnp.clip(jax.random.uniform(seeds[0], (3, N_GX, N_YZ, A), jnp.float32, -0.35, 0.35) * levels(seeds[0], (3, N_GX, N_YZ, A), ((1, 4), (2, 32)), -0.4, 0.0), -0.35, 0.35)
    species = touch_ends(jax.random.randint(seeds[1], (N_GX, N_YZ, A), 0, NSPEC), jax.random.fold_in(seeds[1], 1), 0, NSPEC - 1).astype(jnp.int32)
    neighbors = draw_neighbors(jax.random.fold_in(seeds[11], 71), 0)
    slot_used = draw_slot_used(jax.random.fold_in(seeds[11], 71), 0)
    embed_weight = centred(seeds[4], (NRAD + 2 * NSPEC, LATENT), (NRAD + 2 * NSPEC) ** -0.5, 1.25)
    first_weight = centred(seeds[5], (LATENT, CH), LATENT ** -0.5, 0.5)
    env_weight = centred(seeds[6], (LAYERS, LATENT, CH), LATENT ** -0.5, 0.5)
    latent_weight = centred(seeds[7], (LAYERS, LATENT + 3 * CH, LATENT), (LATENT + 3 * CH) ** -0.5, 0.375)
    mix_weight = centred(seeds[8], (LAYERS - 1, 3, CH, CH), CH ** -0.5, 1.0)
    out_weight = centred(seeds[9], (LATENT, LATENT), LATENT ** -0.5, 0.5)
    out_vector = centred(seeds[10], (LATENT,), LATENT ** -0.5, 0.5, jnp.float32)
    return {"positions": positions, "species": species, "neighbors": neighbors, "slot_used": slot_used, "embed_weight": embed_weight, "first_weight": first_weight, "env_weight": env_weight, "latent_weight": latent_weight, "mix_weight": mix_weight, "out_weight": out_weight, "out_vector": out_vector}


CUTOFF = 5.0
DEGREE_MAP = np.array([0, 1, 1, 1, 2, 2, 2, 2, 2])

def lattice(site_index):
    return (site_index // (LY * LZ), site_index // LZ % LY, site_index % LZ)

def lattice_steps(centre_site, side_gx, side_yz, far_site):
    centre_x, centre_y, centre_z = lattice(centre_site)
    far_x, far_y, far_z = lattice(far_site)
    step_x = (side_gx - 1) * LX + far_x - centre_x[:, None]
    step_y = (side_yz - 1) * LY + far_y - centre_y[:, None]
    step_z = (far_z - centre_z[:, None] + LZ // 2) % LZ - LZ // 2
    return jnp.stack([step_x, step_y, step_z], -1).astype(jnp.float32)

def geometry(displace, in_use):
    length = jnp.sqrt(lax.optimization_barrier(jnp.sum(displace * displace, axis=-1)))
    direct = displace / length[..., None]
    scaled = length / CUTOFF
    envelope = (1.0 - 28.0 * scaled ** 6 + 48.0 * scaled ** 7 - 21.0 * scaled ** 8) * in_use
    orders = jnp.arange(1, NRAD + 1).astype(jnp.float32)
    radial = math.sqrt(2.0 / CUTOFF) * jnp.sin(orders * (math.pi / CUTOFF) * length[..., None]) / length[..., None]
    along_x, along_y, along_z = (direct[..., 0], direct[..., 1], direct[..., 2])
    root_three, root_five, root_fifteen = (math.sqrt(3.0), math.sqrt(5.0), math.sqrt(15.0))
    harmonic = jnp.stack([jnp.ones_like(along_x), root_three * along_x, root_three * along_y, root_three * along_z, root_fifteen * along_x * along_y, root_fifteen * along_y * along_z, 0.5 * root_five * (3.0 * along_z * along_z - 1.0), root_fifteen * along_x * along_z, 0.5 * root_fifteen * (along_x * along_x - along_y * along_y)], -1)
    return jnp.concatenate([radial, harmonic, envelope[..., None]], -1)

def network(features, kind_centre, kind_far, embed_weight, first_weight, env_weight, latent_weight, mix_weight, out_weight, out_vector):
    radial = features[..., :NRAD]
    harmonic = features[..., NRAD:NRAD + 9]
    envelope = features[..., NRAD + 9:NRAD + 10]
    catalog = jnp.arange(NSPEC).astype(jnp.float32)
    centre_hot = (kind_centre[:, None] == catalog).astype(jnp.float32)
    far_hot = (kind_far[..., None] == catalog).astype(jnp.float32)
    inputs = jnp.concatenate([radial, jnp.broadcast_to(centre_hot[:, None, :], far_hot.shape), far_hot], -1)
    latent = jax.nn.silu(jnp.dot(inputs.astype(jnp.bfloat16), embed_weight, preferred_element_type=jnp.float32)) * envelope
    channel_weights = jnp.dot(latent.astype(jnp.bfloat16), first_weight, preferred_element_type=jnp.float32)
    tensor = channel_weights[..., None, :] * harmonic[..., :, None]
    layers = env_weight.shape[0]
    norm_scale = 1.0 / math.sqrt(features.shape[1])
    for layer_no in range(layers):
        env_coeff = jnp.dot(latent.astype(jnp.bfloat16), env_weight[layer_no], preferred_element_type=jnp.float32)
        environ = lax.optimization_barrier(jnp.sum(env_coeff[..., None, :] * harmonic[..., :, None], axis=1, keepdims=True)) * norm_scale
        scalar_zero = tensor[..., 0, :] * environ[..., 0, :]
        scalar_one = lax.optimization_barrier(jnp.sum(tensor[..., 1:4, :] * environ[..., 1:4, :], axis=-2))
        scalar_two = lax.optimization_barrier(jnp.sum(tensor[..., 4:9, :] * environ[..., 4:9, :], axis=-2))
        joined = jnp.concatenate([latent, scalar_zero, scalar_one, scalar_two], -1)
        latent = latent + jax.nn.silu(jnp.dot(joined.astype(jnp.bfloat16), latent_weight[layer_no], preferred_element_type=jnp.float32)) * envelope
        if layer_no + 1 < layers:
            product = tensor * environ[..., 0:1, :] + tensor[..., 0:1, :] * environ
            channel_mix = mix_weight[layer_no].astype(jnp.float32)[DEGREE_MAP]
            tensor = jnp.einsum('cnmk,mkj->cnmj', product, channel_mix, precision=lax.Precision.HIGHEST)
    hidden = jax.nn.silu(jnp.dot(latent.astype(jnp.bfloat16), out_weight, preferred_element_type=jnp.float32))
    pair_energy = lax.optimization_barrier(jnp.sum(hidden * out_vector, axis=-1)) * envelope[..., 0]
    return lax.optimization_barrier(jnp.sum(pair_energy, axis=1))

def pair_terms(displace, in_use, kind_centre, kind_far, params):

    def energy_of(moved):
        return network(geometry(moved, in_use), kind_centre, kind_far, *params)
    energy, pull_back = jax.vjp(energy_of, displace)
    gradient, = pull_back(jnp.ones_like(energy))
    return (energy, gradient)

def reference(positions, species, neighbors, slot_used, embed_weight, first_weight, env_weight, latent_weight, mix_weight, out_weight, out_vector):
    params = (embed_weight, first_weight, env_weight, latent_weight, mix_weight, out_weight, out_vector)
    atom_total = N_GX * N_YZ * A
    listed = neighbors.reshape(atom_total, NB)
    centre = jnp.arange(atom_total, dtype=jnp.int32)
    home_gx = centre // (N_YZ * A)
    home_yz = centre // A % N_YZ
    home_site = centre % A
    side_index = listed // A
    side_gx = side_index // 3
    side_yz = side_index % 3
    far_site = listed % A
    far_gx = (home_gx[:, None] + side_gx - 1) % N_GX
    far_yz = (home_yz[:, None] + side_yz - 1) % N_YZ
    global_far = ((far_gx * N_YZ + far_yz) * A + far_site).astype(jnp.int32)
    offsets = lattice_steps(home_site, side_gx, side_yz, far_site)
    coords = positions.reshape(3, atom_total).T
    displace = coords[global_far] - coords[:, None, :] + offsets
    kind_all = species.reshape(atom_total).astype(jnp.float32)
    kind_far = kind_all[global_far]
    in_use = slot_used.reshape(atom_total, NB).astype(jnp.float32)
    group_size = math.gcd(atom_total, 32)
    groups = atom_total // group_size

    def evaluate(portion):
        return pair_terms(portion[0], portion[1], portion[2], portion[3], params)
    energy, gradient = lax.map(evaluate, (displace.reshape(groups, group_size, NB, 3), in_use.reshape(groups, group_size, NB), kind_all.reshape(groups, group_size), kind_far.reshape(groups, group_size, NB)))
    energy = energy.reshape(atom_total)
    gradient = gradient.reshape(atom_total, NB, 3)
    pulled = jax.ops.segment_sum(gradient.reshape(atom_total * NB, 3), global_far.reshape(-1), num_segments=atom_total)
    forces = (lax.optimization_barrier(jnp.sum(gradient, axis=1)) - pulled).T.reshape(3, N_GX, N_YZ, A)
    return (energy.reshape(N_GX, N_YZ, A), forces)
```

```python
import functools
import math

import jax
import jax.numpy as jnp
import numpy as np
from jax import lax
from jax.experimental import pallas as pl
from jax.experimental.pallas import tpu as pltpu
from jax.sharding import PartitionSpec as P

F32 = jnp.float32
BF16 = jnp.bfloat16
LZ = 8
NRAD = 8
CH = 32
SLOTS = 48
GROUP = 16
PAIRS = GROUP * SLOTS
UNIT = 2
CHUNK = 8
TILE = 256
NORM = 1.0 / math.sqrt(SLOTS)
RADIAL_GAIN = math.sqrt(2.0 / 5.0)
DEGREES = ((0,), (1, 2, 3), (4, 5, 6, 7, 8))
ORDER = (1, 2, 3, 4, 5, 6, 7, 8, 0)
DEGREE_OF = tuple(next(d for d in range(3) if m in DEGREES[d]) for m in ORDER)


def nn(a, b):
    return jnp.dot(a, b, preferred_element_type=F32)


def nt(a, b):
    return lax.dot_general(a, b, (((1,), (1,)), ((), ())), preferred_element_type=F32)


def tn(a, b):
    return lax.dot_general(a, b, (((0,), (0,)), ((), ())), preferred_element_type=F32)


def pieces(value, count):
    out = []
    for _ in range(count):
        part = value.astype(BF16).astype(F32)
        out.append(part)
        value = value - part
    return out


def constants():
    lane = np.arange(PAIRS)
    atom_mask = (lane[None, :] // SLOTS == np.arange(GROUP)[:, None]).astype(np.float32)
    slot_pick = (lane[None, :] % SLOTS == np.arange(SLOTS)[:, None]).astype(np.float32)
    wide = np.arange(GROUP * CH)
    atom_wide = (wide[None, :] // CH == np.arange(GROUP)[:, None]).astype(np.float32)
    chan_wide = (wide[None, :] % CH == np.arange(CH)[:, None]).astype(np.float32)
    degree_mask = np.zeros((96, 144), np.float32)
    for i, d in enumerate(DEGREE_OF):
        degree_mask[d * 32 : d * 32 + 32, i * 16 : i * 16 + 16] = 1.0
    return atom_mask, slot_pick, atom_wide, chan_wide, degree_mask


def geometry(get, put, geo):
    used = get(14) > 0.5
    one = jnp.ones((CHUNK, PAIRS), F32)
    nil = jnp.zeros((CHUNK, PAIRS), F32)
    vx = jnp.where(used, get(0) + (get(3) + get(6)) + get(9), one)
    vy = jnp.where(used, get(1) + (get(4) + get(7)) + get(10), nil)
    step_z = get(11)
    step_z = jnp.where(step_z >= 4.0, step_z - 8.0, jnp.where(step_z < -4.0, step_z + 8.0, step_z))
    vz = jnp.where(used, get(2) + (get(5) + get(8)) + step_z, nil)
    keep = jnp.where(used, one, nil)
    square = vx * vx + vy * vy + vz * vz
    inv = lax.rsqrt(square)
    inv = inv * (1.5 - 0.5 * square * inv * inv)
    length = square * inv
    ux, uy, uz = vx * inv, vy * inv, vz * inv
    t = length * 0.2
    t2 = t * t
    t5 = t2 * t2 * t
    t6 = t5 * t
    envelope = (1.0 - 28.0 * t6 + 48.0 * t6 * t - 21.0 * t6 * t2) * keep
    slope = t5 * (-168.0 + 336.0 * t - 168.0 * t2) * (0.2 * keep)
    y = length * (math.pi / 5.0) - (math.pi / 2.0)
    y2 = y * y
    sine = 1.0 + y2 * (
        -1.0 / 2
        + y2 * (1.0 / 24 + y2 * (-1.0 / 720 + y2 * (1.0 / 40320 + y2 * (-1.0 / 3628800 + y2 * (1.0 / 479001600)))))
    )
    cosine = -y * (
        1.0
        + y2
        * (-1.0 / 6 + y2 * (1.0 / 120 + y2 * (-1.0 / 5040 + y2 * (1.0 / 362880 + y2 * (-1.0 / 39916800)))))
    )
    twice = 2.0 * cosine
    sines, cosines = [nil, sine], [one, cosine]
    for _ in range(NRAD - 1):
        sines.append(twice * sines[-1] - sines[-2])
        cosines.append(twice * cosines[-1] - cosines[-2])
    scale = RADIAL_GAIN * inv
    for n in range(1, NRAD + 1):
        radial = scale * sines[n]
        put(n - 1, radial)
        geo[n - 1] = ((n * math.pi / 5.0) * scale) * cosines[n] - radial * inv
    r3, r5, r15 = math.sqrt(3.0), math.sqrt(5.0), math.sqrt(15.0)
    harmonic = [
        r3 * ux,
        r3 * uy,
        r3 * uz,
        r15 * ux * uy,
        r15 * uy * uz,
        0.5 * r5 * (3.0 * uz * uz - 1.0),
        r15 * ux * uz,
        0.5 * r15 * (ux * ux - uy * uy),
    ]
    for i, value in enumerate(harmonic):
        put(8 + i, value)
    put(16, envelope)
    put(17, get(13))
    put(18, get(12))
    geo[8] = slope
    geo[9] = ux
    geo[10] = uy
    geo[11] = uz
    geo[12] = inv
    geo[13] = keep


def geometry_back(get, put, geo):
    slope, ux, uy, uz, inv, keep = (geo[8 + i] for i in range(6))
    along = get(16) * slope
    for n in range(NRAD):
        along = along + get(n) * geo[n]
    g1, g2, g3, g4, g5, g6, g7, g8 = (get(8 + i) for i in range(8))
    r3, r5, r15 = math.sqrt(3.0), math.sqrt(5.0), math.sqrt(15.0)
    ax = r3 * g1 + r15 * (uy * g4 + uz * g7 + ux * g8)
    ay = r3 * g2 + r15 * (ux * g4 + uz * g5 - uy * g8)
    az = r3 * g3 + r15 * (uy * g5 + ux * g7) + (3.0 * r5) * uz * g6
    radial_part = along - (ax * ux + ay * uy + az * uz) * inv
    for i, (a, u) in enumerate(((ax, ux), (ay, uy), (az, uz))):
        high, low = pieces(jnp.where(keep > 0.5, radial_part * u + a * inv, 0.0), 2)
        put(i, high)
        put(3 + i, low)


def swish(half):
    wide = 1.0 + jnp.tanh(half)
    value = half * wide
    return value, wide + value * (2.0 - wide)


def together(streams):
    while streams:
        left = []
        for stream in streams:
            try:
                next(stream)
                left.append(stream)
            except StopIteration:
                pass
        streams = left


def pair_kernel(
    blocks_ref,
    mid_ref,
    low_ref,
    high_ref,
    neighbors_ref,
    used_ref,
    embed_ref,
    first_ref,
    env_ref,
    latent_ref,
    mix_ref,
    out_ref,
    vector_ref,
    atom_mask_ref,
    slot_pick_ref,
    atom_wide_ref,
    chan_wide_ref,
    degree_mask_ref,
    energy_ref,
    fmid_ref,
    flow_ref,
    fhigh_ref,
    far_tab,
    own_tab,
    ftab,
    embed_t,
    we_t,
    l1_t,
    l2_t,
    e1_t,
    out_t,
    mix_t,
    mix_all,
    mix_wide,
    we_all,
    env1,
    vec_b,
    hot,
    gat,
    feat,
    dfeat,
    geo,
    x0,
    hbd,
    lat,
    dd,
    ss,
    j0,
    j1,
    w_s,
    cat,
    q_s,
    q1_s,
    a_s,
    r_s,
    ds_b,
    dl,
    t_s,
    small,
    dwr,
    e0x,
    e1x,
    bmat,
    eb,
    e0t,
    e1r,
    ww,
    pair_energy,
    db,
    outer,
    de_b,
    left,
):
    def turned(value):
        return value.astype(F32).T

    for ref in (embed_t, l1_t, l2_t, mix_t, mix_all, we_all, env1, eb, e0t, e1r, de_b):
        ref[...] = jnp.zeros_like(ref)
    embed_t[:, 0:24] = (turned(embed_ref[...]) * 0.5).astype(BF16)
    we_t[0:32, :] = turned(first_ref[...]).astype(BF16)
    we_t[32:64, :] = turned(env_ref[0]).astype(BF16)
    e1_t[...] = turned(env_ref[1]).astype(BF16)
    l1_t[:, 0:224] = (turned(latent_ref[0]) * 0.5).astype(BF16)
    l2_t[:, 0:224] = (turned(latent_ref[1]) * 0.5).astype(BF16)
    out_t[...] = (turned(out_ref[...]) * 0.5).astype(BF16)
    we_all[:, 0:64] = jnp.concatenate([first_ref[...], env_ref[0]], axis=1)
    env1[:, 0:32] = env_ref[1]
    mix_all[:, 0:96] = jnp.concatenate([mix_ref[d] for d in range(3)], axis=1)
    for d in range(3):
        mix_t[32 * d : 32 * d + 32, 0:32] = turned(mix_ref[d]).astype(BF16)
    mix_wide[...] = nn(mix_t[:, 0:32], chan_wide_ref[...])
    vec_b[...] = jnp.broadcast_to(vector_ref[...].T, (128, TILE))

    def enter(values_ref, per_plane, first_y):
        count = values_ref.shape[1]
        lane = lax.broadcasted_iota(jnp.int32, (1, count), 1)
        plane = lane // per_plane
        rest = lane - plane * per_plane
        column = rest // LZ
        lattice = [plane.astype(F32), (column + first_y).astype(F32), (rest - column * LZ).astype(F32)]
        xyz = values_ref[0:3, :]
        kind = values_ref[3:4, :]
        one = jnp.ones((1, count), F32)
        nil = jnp.zeros((1, count), F32)
        places = jnp.concatenate(pieces(xyz, 3) + lattice, axis=0)
        far = jnp.concatenate([places, kind, nil, one, nil], axis=0).T.astype(BF16)
        own = jnp.concatenate([-places, nil, kind, nil, nil], axis=0).T.astype(BF16)
        for p in range(12):
            start = p * 96 + first_y * LZ
            far_tab[start : start + per_plane, :] = far[p * per_plane : (p + 1) * per_plane, :]
            own_tab[start : start + per_plane, :] = own[p * per_plane : (p + 1) * per_plane, :]

    enter(mid_ref, 64, 2)
    enter(low_ref, 16, 0)
    enter(high_ref, 16, 10)
    ftab[...] = jnp.zeros_like(ftab)
    energy_ref[...] = jnp.zeros_like(energy_ref)
    gat[...] = jnp.zeros_like(gat)
    dfeat[...] = jnp.zeros_like(dfeat)
    hot_rows = lax.broadcasted_iota(jnp.int32, (240, PAIRS), 0).astype(F32)
    tiles = [slice(TILE * j, TILE * j + TILE) for j in range(PAIRS // TILE)]
    halves = [slice(0, 384), slice(384, 768)]
    wides = [slice(0, 256), slice(256, 512)]

    def row_base(block):
        return (block // 4) * 96 + (block % 4) * 16

    def fetch(block, slot):
        x = block // 4
        yb = block % 4
        rows = pl.ds(pl.multiple_of(block * GROUP, GROUP), GROUP)
        name = neighbors_ref[rows, :]
        side = name >> 9
        site = name & 511
        a = (side * 11) >> 5
        c = side - 3 * a
        ex = a * 8 + (site >> 6) - 6 - x
        ey = c * 8 + ((site >> 3) & 7) - 6 - 2 * yb
        local = ex * 48 + ey * 8 + (site & 7)
        local = jnp.where(used_ref[rows, :] > 0, local, -1)
        spread = nn(local.astype(F32).astype(BF16), slot_pick_ref[...])
        index = jnp.sum(spread * atom_mask_ref[...].astype(F32), axis=0, keepdims=True)
        hot[slot, 0:240, :] = jnp.where(hot_rows == index, 1.0, 0.0).astype(BF16)
        hot[slot, 240:256, :] = atom_mask_ref[...]
        base = row_base(block)
        parts = [far_tab[pl.ds(pl.multiple_of(base + 96 * i, 16), 48), :] for i in range(5)]
        parts.append(own_tab[pl.ds(pl.multiple_of(base + 208, 16), 16), :])
        table = jnp.concatenate(parts, axis=0)
        gat[slot] = tn(table, hot[slot])

    def network(block, slot):
        mask = atom_mask_ref[...].astype(F32)
        wide_mask = atom_wide_ref[...].astype(F32)

        def prepare(k):
            species_row = lax.broadcasted_iota(jnp.int32, (8, PAIRS), 0).astype(F32)
            hot_own = jnp.where(species_row == feat[slot + k, 17:18, :], 1.0, 0.0)
            hot_far = jnp.where(species_row == feat[slot + k, 18:19, :], 1.0, 0.0)
            nil = jnp.zeros((8, PAIRS), F32)
            x0[k] = jnp.concatenate([feat[slot + k, 0:8, :], hot_own, hot_far, nil], axis=0).astype(BF16)
            for i in range(8):
                hbd[k, 16 * i : 16 * i + 16, :] = (feat[slot + k, 8 + i : 9 + i, :] * mask).astype(BF16)
            hbd[k, 128:144, :] = atom_mask_ref[...]
            yield

        def env(k, cols):
            return feat[slot + k, 16:17, cols]

        sums = {}

        def gather_sum(key, part):
            sums[key] = sums[key] + part if key in sums else part

        def stage_a(k, cols):
            half = nn(embed_t[:, 0:32], x0[k, :, cols])
            yield
            value, slope = swish(half)
            ss[k, 0, :, cols] = value
            dd[k, 0, :, cols] = slope * (0.5 * env(k, cols))
            latent = value * env(k, cols)
            lat[k, 0, :, cols] = latent
            packed = latent.astype(BF16)
            j0[k, 0:128, cols] = packed
            we = nn(we_t[...], packed)
            yield
            w_s[k, :, cols] = we[0:32]
            coeff = we[32:64].astype(BF16)
            cat[k, 224:256, cols] = coeff
            gather_sum(("e0", k), nt(coeff, hbd[k, :, cols]))
            yield

        def between_a(k):
            environ = sums["e0", k] * NORM
            sums["e0", k] = environ
            eb[k, 0, :, 0:144] = (jnp.concatenate([environ] * 3, axis=0) * degree_mask_ref[...]).astype(BF16)
            e0t[k, :, 0:32] = environ.T.astype(BF16)
            yield
            spread = nn(e0t[k, :, 0:32], chan_wide_ref[...])
            yield
            for i in range(9):
                e0x[k, i : i + 1, :] = jnp.sum(
                    spread[16 * i : 16 * i + 16, :] * wide_mask, axis=0, keepdims=True
                )

        def stage_b(k, cols):
            q = nn(eb[k, 0, :, 0:144], hbd[k, :, cols])
            yield
            q_s[k, :, cols] = q
            w3 = jnp.concatenate([w_s[k, :, cols]] * 3, axis=0)
            scal = (q * w3).astype(BF16)
            j0[k, 128:224, cols] = scal
            half = nn(l1_t[:, 0:224], j0[k, :, cols])
            mixed = nn(mix_t[:, 0:32], scal[0:32])
            yield
            a_s[k, :, cols] = mixed
            value, slope = swish(half)
            ss[k, 1, :, cols] = value
            dd[k, 1, :, cols] = slope * (0.5 * env(k, cols))
            latent = lat[k, 0, :, cols] + value * env(k, cols)
            lat[k, 1, :, cols] = latent
            packed = latent.astype(BF16)
            j1[k, 0:128, cols] = packed
            coeff = nn(e1_t[...], packed)
            yield
            coeff = coeff.astype(BF16)
            cat[k, 192:224, cols] = coeff
            gather_sum(("e1", k), nt(coeff, hbd[k, :, cols]))
            yield

        def spread_w(k, half):
            w = w_s[k, :, halves[half]]
            m8 = mask[8 * half : 8 * half + 8, halves[half]]
            return jnp.concatenate([w * m8[p : p + 1, :] for p in range(8)], axis=0).astype(BF16)

        def stage_c(k):
            environ = sums["e1", k] * NORM
            sums["e1", k] = environ
            eb[k, 1, :, 0:144] = (jnp.concatenate([environ] * 3, axis=0) * degree_mask_ref[...]).astype(BF16)
            e1r[k, :, 0:16] = jnp.concatenate(
                [environ[:, 16 * i : 16 * i + 16] for i in range(9)], axis=0
            ).astype(BF16)
            yield
            for i in range(9):
                e1x[k, 32 * i : 32 * i + 32, :] = nn(e1r[k, 32 * i : 32 * i + 32, 0:16], atom_wide_ref[...])
            for half in range(2):
                ww[k, half] = spread_w(k, half)
            yield
            for d in range(3):
                total = None
                for i in range(9):
                    if DEGREE_OF[i] == d:
                        part = e1x[k, 32 * i : 32 * i + 32, :] * e0x[k, i : i + 1, :]
                        total = part if total is None else total + part
                rows = slice(32 * d, 32 * d + 32)
                bmat[k, rows, :] = (total * mix_wide[rows, :]).astype(BF16)
            yield
            for half in range(2):
                r_s[k, :, halves[half]] = nn(bmat[k, :, wides[half]], ww[k, half])
            yield

        def stage_d(k, cols):
            q = nn(eb[k, 1, :, 0:144], hbd[k, :, cols])
            yield
            a = a_s[k, :, cols]
            q1_s[k, :, cols] = q
            j1[k, 128:224, cols] = (a * q + r_s[k, :, cols]).astype(BF16)
            half = nn(l2_t[:, 0:224], j1[k, :, cols])
            yield
            value, slope = swish(half)
            ss[k, 2, :, cols] = value
            dd[k, 2, :, cols] = slope * (0.5 * env(k, cols))
            latent = lat[k, 1, :, cols] + value * env(k, cols)
            half = nn(out_t[...], latent.astype(BF16))
            yield
            hidden, slope = swish(half)
            weighted = hidden * vec_b[...]
            t_s[k, :, cols] = weighted
            dz3 = (slope * vec_b[...] * (0.5 * env(k, cols))).astype(BF16)
            dl2 = nn(out_ref[...], dz3)
            pair_energy[k, :, cols] = jnp.sum(weighted, axis=0, keepdims=True) * env(k, cols)
            yield
            t_s[k, :, cols] = t_s[k, :, cols] + dl2 * ss[k, 2, :, cols]
            dl[k, :, cols] = dl2
            dj = nn(latent_ref[1], (dl2 * dd[k, 2, :, cols]).astype(BF16))
            yield
            dl[k, :, cols] = dl[k, :, cols] + dj[0:128]
            dscal = dj[128:224]
            ds_b[k, :, cols] = dscal.astype(BF16)
            dmix = nn(mix_all[:, 0:96], (dscal * q1_s[k, :, cols]).astype(BF16))
            dq = (dscal * a_s[k, :, cols]).astype(BF16)
            cat[k, 0:96, cols] = dq
            gather_sum(("d1", k), nt(dq, hbd[k, :, cols]))
            yield
            small[k, :, cols] = dmix

        def stage_e(k):
            row = pair_energy[k]
            high, middle, low = pieces(row, 3)
            fill = jnp.zeros((5, PAIRS), F32)
            total = nt(jnp.concatenate([high, middle, low, fill], axis=0).astype(BF16), atom_mask_ref[...])
            energy_ref[pl.ds(block + k, 1), :] = total[0:1] + (total[1:2] + total[2:3])
            for half in range(2):
                db[k, :, wides[half]] = nt(ds_b[k, :, halves[half]], ww[k, half])
                back = tn(bmat[k, :, wides[half]], ds_b[k, :, halves[half]])
                m8 = mask[8 * half : 8 * half + 8, halves[half]]
                total = back[0:32] * m8[0:1]
                for p in range(1, 8):
                    total = total + back[32 * p : 32 * p + 32] * m8[p : p + 1]
                dwr[k, :, halves[half]] = total
            yield
            inner = []
            for i in range(9):
                rows = slice(32 * DEGREE_OF[i], 32 * DEGREE_OF[i] + 32)
                piece = db[k, rows, :] * mix_wide[rows, :]
                outer[k, 32 * i : 32 * i + 32, :] = (piece * e0x[k, i : i + 1, :]).astype(BF16)
                inner.append(jnp.sum(piece * e1x[k, 32 * i : 32 * i + 32, :], axis=0, keepdims=True))
            yield
            side = nt(outer[k], atom_wide_ref[...])
            de0t = nt(jnp.concatenate([r * wide_mask for r in inner], axis=0).astype(BF16), chan_wide_ref[...])
            yield
            de = sums["d1", k] * degree_mask_ref[...]
            de = de[0:32] + de[32:64] + de[64:96]
            de = de + jnp.concatenate([side[32 * i : 32 * i + 32, :] for i in range(9)], axis=1)
            de = de * NORM
            sums["d1", k] = de
            de_b[k, 1, :, 0:144] = de.astype(BF16)
            sums["side0", k] = de0t.T

        def stage_f(k, cols):
            dcoeff = nn(de_b[k, 1, :, 0:144], hbd[k, :, cols])
            yield
            more = nn(env1[:, 0:32], dcoeff.astype(BF16))
            yield
            dl1 = dl[k, :, cols] + more
            t_s[k, :, cols] = t_s[k, :, cols] + dl1 * ss[k, 1, :, cols]
            dl[k, :, cols] = dl1
            dj = nn(latent_ref[0], (dl1 * dd[k, 1, :, cols]).astype(BF16))
            yield
            dl[k, :, cols] = dl[k, :, cols] + dj[0:128]
            dscal = [dj[128:160] + small[k, :, cols], dj[160:192], dj[192:224]]
            w = w_s[k, :, cols]
            dw = dwr[k, :, cols]
            for d in range(3):
                cat[k, 96 + 32 * d : 128 + 32 * d, cols] = (dscal[d] * w).astype(BF16)
                dw = dw + dscal[d] * q_s[k, 32 * d : 32 * d + 32, cols]
            dwr[k, :, cols] = dw
            gather_sum(("d0", k), nt(cat[k, 96:192, cols], hbd[k, :, cols]))
            yield

        def between_f(k):
            de = sums["d0", k] * degree_mask_ref[...]
            de = (de[0:32] + de[32:64] + de[64:96] + sums["side0", k]) * NORM
            de_b[k, 0, :, 0:144] = de.astype(BF16)
            yield
            e0, e1, d1 = sums["e0", k], sums["e1", k], sums["d1", k]
            tall = []
            for e in (e1, e0):
                three = jnp.concatenate([e[:, 0:128]] * 3, axis=0)
                tall.append(three * degree_mask_ref[:, 0:128])
            tall += [d1[:, 0:128], de[:, 0:128]]
            left[k] = jnp.concatenate(tall, axis=0).T.astype(BF16)
            yield

        def stage_h(k, cols):
            dcoeff = nn(de_b[k, 0, :, 0:144], hbd[k, :, cols])
            dhbd = nn(left[k], cat[k, :, cols])
            yield
            both = jnp.concatenate([dwr[k, :, cols], dcoeff], axis=0).astype(BF16)
            more = nn(we_all[:, 0:64], both)
            for i in range(8):
                dfeat[slot + k, 8 + i : 9 + i, cols] = jnp.sum(
                    dhbd[16 * i : 16 * i + 16, :] * mask[:, cols], axis=0, keepdims=True
                )
            yield
            so_far = dl[k, :, cols]
            dl0 = jnp.where(jnp.abs(so_far) < 1e30, so_far, 0.0) + more
            dz = (dl0 * dd[k, 0, :, cols]).astype(BF16)
            dradial = nn(embed_ref[...], dz)
            dfeat[slot + k, 16:17, cols] = jnp.sum(
                t_s[k, :, cols] + dl0 * ss[k, 0, :, cols], axis=0, keepdims=True
            )
            yield
            dfeat[slot + k, 0:8, cols] = dradial[0:8]

        members = range(UNIT)
        for stage, tiled in (
            (prepare, False),
            (stage_a, True),
            (between_a, False),
            (stage_b, True),
            (stage_c, False),
            (stage_d, True),
            (stage_e, False),
            (stage_f, True),
            (between_f, False),
            (stage_h, True),
        ):
            if tiled:
                together([stage(k, cols) for k in members for cols in tiles])
            else:
                together([stage(k) for k in members])

    def scatter(block, slot):
        pulled = nt(hot[slot], dfeat[slot, 0:16, :].astype(BF16))
        base = row_base(block)
        for i in range(5):
            rows = pl.ds(pl.multiple_of(base + 96 * i, 16), 48)
            ftab[rows, :] = ftab[rows, :] - pulled[48 * i : 48 * i + 48, :]
        rows = pl.ds(pl.multiple_of(base + 208, 16), 16)
        ftab[rows, :] = ftab[rows, :] + pulled[240:256, :]

    blocks = ((blocks_ref[0] + UNIT - 1) // UNIT) * UNIT

    def chunk_step(chunk, carry):
        first = chunk * CHUNK
        count = jnp.minimum(CHUNK, blocks - first)

        def rows_of(ref):
            return lambda f: jnp.concatenate([ref[b, f : f + 1, :] for b in range(CHUNK)], axis=0)

        def rows_to(ref):
            def put(f, value):
                for b in range(CHUNK):
                    ref[b, f : f + 1, :] = value[b : b + 1, :]

            return put

        def each(step, size=1):
            def turn(i, c):
                step(first + i * size, i * size)
                return c

            lax.fori_loop(0, (count + size - 1) // size, turn, 0)

        each(fetch)
        geometry(rows_of(gat), rows_to(feat), geo)
        each(network, UNIT)
        geometry_back(rows_of(dfeat), rows_to(dfeat), geo)
        each(scatter)
        return carry

    lax.fori_loop(0, (blocks + CHUNK - 1) // CHUNK, chunk_step, 0)

    def leave(force_ref, per_plane, first_y):
        rows = jnp.concatenate(
            [ftab[p * 96 + first_y * LZ : p * 96 + first_y * LZ + per_plane, :] for p in range(12)], axis=0
        )
        turned_rows = rows.T
        force_ref[...] = turned_rows[0:3] + turned_rows[3:6]

    leave(fmid_ref, 64, 2)
    leave(flow_ref, 16, 0)
    leave(fhigh_ref, 16, 10)


def pair_call(blocks, mid, low, high, neighbors, used, params):
    embed, first, env, latent, mix, out, vector = params
    sites = neighbors.shape[0]
    atom_mask, slot_pick, atom_wide, chan_wide, degree_mask = constants()
    consts = [
        jnp.asarray(atom_mask, BF16),
        jnp.asarray(slot_pick, BF16),
        jnp.asarray(atom_wide, BF16),
        jnp.asarray(chan_wide, BF16),
        jnp.asarray(degree_mask, F32),
    ]
    vm = pl.BlockSpec(memory_space=pltpu.VMEM)
    sm = pl.BlockSpec(memory_space=pltpu.SMEM)
    scratch = [
        ((1152, 16), BF16),
        ((1152, 16), BF16),
        ((1152, 16), F32),
        ((128, 128), BF16),
        ((64, 128), BF16),
        ((128, 256), BF16),
        ((128, 256), BF16),
        ((32, 128), BF16),
        ((128, 128), BF16),
        ((96, 128), BF16),
        ((32, 128), BF16),
        ((96, 512), F32),
        ((128, 128), BF16),
        ((128, 128), BF16),
        ((128, TILE), F32),
        ((CHUNK, 256, PAIRS), BF16),
        ((CHUNK, 16, PAIRS), F32),
        ((CHUNK, 24, PAIRS), F32),
        ((CHUNK, 24, PAIRS), F32),
        ((14, CHUNK, PAIRS), F32),
        ((UNIT, 32, PAIRS), BF16),
        ((UNIT, 144, PAIRS), BF16),
        ((UNIT, 2, 128, PAIRS), F32),
        ((UNIT, 3, 128, PAIRS), F32),
        ((UNIT, 3, 128, PAIRS), F32),
        ((UNIT, 224, PAIRS), BF16),
        ((UNIT, 224, PAIRS), BF16),
        ((UNIT, 32, PAIRS), F32),
        ((UNIT, 256, PAIRS), BF16),
        ((UNIT, 96, PAIRS), F32),
        ((UNIT, 96, PAIRS), F32),
        ((UNIT, 96, PAIRS), F32),
        ((UNIT, 96, PAIRS), F32),
        ((UNIT, 96, PAIRS), BF16),
        ((UNIT, 128, PAIRS), F32),
        ((UNIT, 128, PAIRS), F32),
        ((UNIT, 32, PAIRS), F32),
        ((UNIT, 32, PAIRS), F32),
        ((UNIT, 16, 512), F32),
        ((UNIT, 288, 512), F32),
        ((UNIT, 96, 512), BF16),
        ((UNIT, 2, 96, 256), BF16),
        ((UNIT, 144, 128), BF16),
        ((UNIT, 288, 128), BF16),
        ((UNIT, 2, 256, 384), BF16),
        ((UNIT, 1, PAIRS), F32),
        ((UNIT, 96, 512), F32),
        ((UNIT, 288, 512), BF16),
        ((UNIT, 2, 32, 256), BF16),
        ((UNIT, 128, 256), BF16),
    ]
    return pl.pallas_call(
        pair_kernel,
        out_shape=[
            jax.ShapeDtypeStruct((sites // GROUP, GROUP), F32),
            jax.ShapeDtypeStruct((3, 768), F32),
            jax.ShapeDtypeStruct((3, 192), F32),
            jax.ShapeDtypeStruct((3, 192), F32),
        ],
        in_specs=[sm] + [vm] * 17,
        out_specs=[vm] * 4,
        scratch_shapes=[pltpu.VMEM(shape, dtype) for shape, dtype in scratch],
        compiler_params=pltpu.CompilerParams(vmem_limit_bytes=48 * 1024 * 1024),
        name="pair_terms",
    )(blocks, mid, low, high, neighbors, used, embed, first, env, latent, mix[0], out, vector.reshape(1, -1), *consts)


def shift_pairs(axis, by):
    count = lax.axis_size(axis)
    return [(i, (i + by) % count) for i in range(count)]


def on_device(positions, species, neighbors, slot_used, *params):
    sites = species.shape[-1]
    near = neighbors.reshape(sites, SLOTS)
    used = slot_used.reshape(sites, SLOTS)
    own = jnp.concatenate(
        [positions.reshape(3, sites), species.reshape(1, sites).astype(F32)], axis=0
    )
    up_x, down_x = shift_pairs("gx", 1), shift_pairs("gx", -1)
    up_y, down_y = shift_pairs("yz", 1), shift_pairs("yz", -1)
    before = lax.ppermute(own[:, 384:512], "gx", up_x)
    after = lax.ppermute(own[:, 0:128], "gx", down_x)
    mid = jnp.concatenate([before, own, after], axis=1)
    planes = mid.reshape(4, 12, 64)
    low = lax.ppermute(planes[:, :, 48:64].reshape(4, 192), "yz", up_y)
    high = lax.ppermute(planes[:, :, 0:16].reshape(4, 192), "yz", down_y)
    filled = jnp.max(jnp.where(used > 0, lax.broadcasted_iota(jnp.int32, used.shape, 0) + 1, 0))
    blocks = ((filled + GROUP - 1) // GROUP).reshape(1)
    energy, fmid, flow, fhigh = pair_call(blocks, mid, low, high, near, used, params)
    from_high = lax.ppermute(flow, "yz", down_y).reshape(3, 12, 16)
    from_low = lax.ppermute(fhigh, "yz", up_y).reshape(3, 12, 16)
    gap = jnp.zeros((3, 12, 32), F32)
    column = fmid + jnp.concatenate([from_low, gap, from_high], axis=2).reshape(3, 768)
    from_after = lax.ppermute(column[:, 0:128], "gx", down_x)
    from_before = lax.ppermute(column[:, 640:768], "gx", up_x)
    gap = jnp.zeros((3, 256), F32)
    forces = column[:, 128:640] + jnp.concatenate([from_before, gap, from_after], axis=1)
    return (energy.reshape(1, 1, sites), forces.reshape(3, 1, 1, sites))


def solution(mesh):
    in_specs = (
        P(None, "gx", "yz", None),
        P("gx", "yz", None),
        P("gx", "yz", None, None),
        P("gx", "yz", None, None),
        P(),
        P(),
        P(),
        P(),
        P(),
        P(),
        P(),
    )
    out_specs = (P("gx", "yz", None), P(None, "gx", "yz", None))
    return jax.shard_map(
        on_device, mesh=mesh, in_specs=in_specs, out_specs=out_specs, check_vma=False
    )
```

```python
import functools
import math

import jax
import jax.numpy as jnp
import numpy as np
from jax import lax
from jax.experimental import pallas as pl
from jax.experimental.pallas import tpu as pltpu
from jax.sharding import PartitionSpec as P

F32 = jnp.float32
BF16 = jnp.bfloat16
LZ = 8
NRAD = 8
CH = 32
SLOTS = 48
GROUP = 16
PAIRS = GROUP * SLOTS
UNIT = 7
CHUNK = UNIT
TILE = 256
KEPT = 14
LENT = 6
LIGHT_BLOCKS = 8
SHARE = 144
BOX = 2304
NORM = 1.0 / math.sqrt(SLOTS)
RADIAL_GAIN = math.sqrt(2.0 / 5.0)
DEGREES = ((0,), (1, 2, 3), (4, 5, 6, 7, 8))
ORDER = (1, 2, 3, 4, 5, 6, 7, 8, 0)
DEGREE_OF = tuple(next(d for d in range(3) if m in DEGREES[d]) for m in ORDER)


def nn(a, b):
    return jnp.dot(a, b, preferred_element_type=F32)


def nt(a, b):
    return lax.dot_general(a, b, (((1,), (1,)), ((), ())), preferred_element_type=F32)


def tn(a, b):
    return lax.dot_general(a, b, (((0,), (0,)), ((), ())), preferred_element_type=F32)


def eighth(value):
    return jnp.sum(value.reshape(value.shape[0] // 8, 8, value.shape[1]), axis=0)


def pieces(value, count):
    out = []
    for _ in range(count):
        part = value.astype(BF16).astype(F32)
        out.append(part)
        value = value - part
    return out


def constants():
    lane = np.arange(PAIRS)
    atom_mask = (lane[None, :] // SLOTS == np.arange(GROUP)[:, None]).astype(np.float32)
    slot_pick = (lane[None, :] % SLOTS == np.arange(SLOTS)[:, None]).astype(np.float32)
    wide = np.arange(GROUP * CH)
    atom_wide = (wide[None, :] // CH == np.arange(GROUP)[:, None]).astype(np.float32)
    chan_wide = (wide[None, :] % CH == np.arange(CH)[:, None]).astype(np.float32)
    degree_mask = np.zeros((96, 144), np.float32)
    for i, d in enumerate(DEGREE_OF):
        degree_mask[d * 32 : d * 32 + 32, i * 16 : i * 16 + 16] = 1.0
    return atom_mask, slot_pick, atom_wide, chan_wide, degree_mask


def geometry(get, put, geo):
    used = get(14) > 0.5
    one = jnp.ones((CHUNK, PAIRS), F32)
    nil = jnp.zeros((CHUNK, PAIRS), F32)
    vx = jnp.where(used, get(0) + (get(3) + get(6)) + get(9), one)
    vy = jnp.where(used, get(1) + (get(4) + get(7)) + get(10), nil)
    step_z = get(11)
    step_z = jnp.where(step_z >= 4.0, step_z - 8.0, jnp.where(step_z < -4.0, step_z + 8.0, step_z))
    vz = jnp.where(used, get(2) + (get(5) + get(8)) + step_z, nil)
    keep = jnp.where(used, one, nil)
    square = vx * vx + vy * vy + vz * vz
    inv = lax.rsqrt(square)
    inv = inv * (1.5 - 0.5 * square * inv * inv)
    length = square * inv
    ux, uy, uz = vx * inv, vy * inv, vz * inv
    t = length * 0.2
    t2 = t * t
    t5 = t2 * t2 * t
    t6 = t5 * t
    envelope = (1.0 - 28.0 * t6 + 48.0 * t6 * t - 21.0 * t6 * t2) * keep
    slope = t5 * (-168.0 + 336.0 * t - 168.0 * t2) * (0.2 * keep)
    y = length * (math.pi / 5.0) - (math.pi / 2.0)
    y2 = y * y
    sine = 1.0 + y2 * (
        -1.0 / 2
        + y2 * (1.0 / 24 + y2 * (-1.0 / 720 + y2 * (1.0 / 40320 + y2 * (-1.0 / 3628800 + y2 * (1.0 / 479001600)))))
    )
    cosine = -y * (
        1.0
        + y2
        * (-1.0 / 6 + y2 * (1.0 / 120 + y2 * (-1.0 / 5040 + y2 * (1.0 / 362880 + y2 * (-1.0 / 39916800)))))
    )
    twice = 2.0 * cosine
    sines, cosines = [nil, sine], [one, cosine]
    for _ in range(NRAD - 1):
        sines.append(twice * sines[-1] - sines[-2])
        cosines.append(twice * cosines[-1] - cosines[-2])
    scale = RADIAL_GAIN * inv
    for n in range(1, NRAD + 1):
        radial = scale * sines[n]
        put(n - 1, radial)
        geo[n - 1] = ((n * math.pi / 5.0) * scale) * cosines[n] - radial * inv
    r3, r5, r15 = math.sqrt(3.0), math.sqrt(5.0), math.sqrt(15.0)
    harmonic = [
        r3 * ux,
        r3 * uy,
        r3 * uz,
        r15 * ux * uy,
        r15 * uy * uz,
        0.5 * r5 * (3.0 * uz * uz - 1.0),
        r15 * ux * uz,
        0.5 * r15 * (ux * ux - uy * uy),
    ]
    for i, value in enumerate(harmonic):
        put(8 + i, value)
    put(16, envelope)
    put(17, get(13))
    put(18, get(12))
    geo[8] = slope
    geo[9] = ux
    geo[10] = uy
    geo[11] = uz
    geo[12] = inv
    geo[13] = keep


def geometry_back(get, put, geo):
    slope, ux, uy, uz, inv, keep = (geo[8 + i] for i in range(6))
    along = get(16) * slope
    for n in range(NRAD):
        along = along + get(n) * geo[n]
    g1, g2, g3, g4, g5, g6, g7, g8 = (get(8 + i) for i in range(8))
    r3, r5, r15 = math.sqrt(3.0), math.sqrt(5.0), math.sqrt(15.0)
    ax = r3 * g1 + r15 * (uy * g4 + uz * g7 + ux * g8)
    ay = r3 * g2 + r15 * (ux * g4 + uz * g5 - uy * g8)
    az = r3 * g3 + r15 * (uy * g5 + ux * g7) + (3.0 * r5) * uz * g6
    radial_part = along - (ax * ux + ay * uy + az * uz) * inv
    for i, (a, u) in enumerate(((ax, ux), (ay, uy), (az, uz))):
        high, low = pieces(jnp.where(keep > 0.5, radial_part * u + a * inv, 0.0), 2)
        put(i, high)
        put(3 + i, low)


def swish(half):
    wide = 1.0 + jnp.tanh(half)
    value = half * wide
    return value, wide + value * (2.0 - wide)


def together(streams):
    while streams:
        left = []
        for stream in streams:
            try:
                next(stream)
                left.append(stream)
            except StopIteration:
                pass
        streams = left


def pair_kernel(
    blocks_ref,
    mid_ref,
    low_ref,
    high_ref,
    neighbors_ref,
    used_ref,
    lent_ref,
    lent_sites_ref,
    embed_ref,
    first_ref,
    env_ref,
    latent_ref,
    mix_ref,
    out_ref,
    vector_ref,
    atom_mask_ref,
    slot_pick_ref,
    atom_wide_ref,
    chan_wide_ref,
    degree_mask_ref,
    energy_ref,
    fmid_ref,
    flow_ref,
    fhigh_ref,
    flent_ref,
    codes,
    far_tab,
    own_tab,
    ftab,
    embed_t,
    we_t,
    l1_t,
    l2_t,
    e1_t,
    out_t,
    mix_t,
    mix_all,
    mix_wide,
    vec_b,
    hot,
    gat,
    feat,
    dfeat,
    geo,
    x0,
    hbd,
    dd,
    ss,
    j0,
    j1,
    w_s,
    cat,
    q_s,
    q1_s,
    a_s,
    r_s,
    ds_b,
    t_s,
    small,
    dwr,
    e0x,
    e1x,
    bmat,
    eb,
    e0t,
    e1r,
    ww,
    pair_energy,
    db,
    outer,
    de_b,
    left,
    dzs,
    back_w,
):
    def turned(value):
        return value.astype(F32).T

    for ref in (embed_t, l1_t, l2_t, mix_t, mix_all, back_w, eb, e0t, e1r, de_b):
        ref[...] = jnp.zeros_like(ref)
    embed_t[:, 0:24] = (turned(embed_ref[...]) * 0.5).astype(BF16)
    we_t[0:32, :] = turned(first_ref[...]).astype(BF16)
    we_t[32:64, :] = turned(env_ref[0]).astype(BF16)
    e1_t[...] = turned(env_ref[1]).astype(BF16)
    l1_t[:, 0:224] = (turned(latent_ref[0]) * 0.5).astype(BF16)
    l2_t[:, 0:224] = (turned(latent_ref[1]) * 0.5).astype(BF16)
    out_t[...] = (turned(out_ref[...]) * 0.5).astype(BF16)
    back_w[:, 0:480] = jnp.concatenate(
        [out_ref[...], latent_ref[1, 0:128], env_ref[1], latent_ref[0, 0:128], first_ref[...], env_ref[0]],
        axis=1,
    )
    mix_all[:, 0:96] = jnp.concatenate([mix_ref[d] for d in range(3)], axis=1)
    for d in range(3):
        mix_t[32 * d : 32 * d + 32, 0:32] = turned(mix_ref[d]).astype(BF16)
    mix_wide[...] = nn(mix_t[:, 0:32], chan_wide_ref[...])
    vec_b[...] = jnp.broadcast_to(vector_ref[...].T, (128, TILE))

    def enter(values_ref, per_plane, first_y, planes=12, first_row=0):
        count = values_ref.shape[1]
        lane = lax.broadcasted_iota(jnp.int32, (1, count), 1)
        plane = lane // per_plane
        rest = lane - plane * per_plane
        column = rest // LZ
        lattice = [plane.astype(F32), (column + first_y).astype(F32), (rest - column * LZ).astype(F32)]
        xyz = values_ref[0:3, :]
        kind = values_ref[3:4, :]
        one = jnp.ones((1, count), F32)
        nil = jnp.zeros((1, count), F32)
        places = jnp.concatenate(pieces(xyz, 3) + lattice, axis=0)
        far = jnp.concatenate([places, kind, nil, one, nil], axis=0).T.astype(BF16)
        own = jnp.concatenate([-places, nil, kind, nil, nil], axis=0).T.astype(BF16)
        for p in range(planes):
            start = first_row + p * 96 + first_y * LZ
            far_tab[start : start + per_plane, :] = far[p * per_plane : (p + 1) * per_plane, :]
            own_tab[start : start + per_plane, :] = own[p * per_plane : (p + 1) * per_plane, :]

    enter(mid_ref, 64, 2)
    enter(low_ref, 16, 0)
    enter(high_ref, 16, 10)
    enter(lent_sites_ref, 96, 0, 6, 1152)
    codes[0:512, :] = jnp.where(used_ref[...] > 0, neighbors_ref[...], -1)
    codes[512:608, :] = lent_ref[...].astype(jnp.int32)
    ftab[...] = jnp.zeros_like(ftab)
    energy_ref[...] = jnp.zeros_like(energy_ref)
    gat[...] = jnp.zeros_like(gat)
    dfeat[...] = jnp.zeros_like(dfeat)
    hot_rows = lax.broadcasted_iota(jnp.int32, (240, PAIRS), 0).astype(F32)
    tiles = [slice(TILE * j, TILE * j + TILE) for j in range(PAIRS // TILE)]
    halves = [slice(0, 384), slice(384, 768)]
    wides = [slice(0, 256), slice(256, 512)]

    own_blocks, lent_blocks, lent_first = blocks_ref[0], blocks_ref[1], blocks_ref[2]

    def place(block):
        step = block - own_blocks
        lent = step >= 0
        step = jnp.minimum(step, LENT - 1)
        home = jnp.where(lent, lent_first + step, block)
        plane = home // 4 - jnp.where(lent, lent_first // 4 - 12, 0)
        base = plane * 96 + (home % 4) * 16
        row = jnp.where(block < own_blocks + lent_blocks, jnp.where(lent, 32 + step, home), 39)
        return home, base, jnp.where(lent, 512 + step * GROUP, home * GROUP), row

    def fetch(block, slot):
        home, base, code_row, _ = place(block)
        x = home // 4
        yb = home % 4
        name = codes[pl.ds(pl.multiple_of(code_row, GROUP), GROUP), :]
        present = (name >= 0) & (block < own_blocks + lent_blocks)
        name = jnp.where(present, name, 0)
        side = name >> 9
        site = name & 511
        a = (side * 11) >> 5
        c = side - 3 * a
        ex = a * 8 + (site >> 6) - 6 - x
        ey = c * 8 + ((site >> 3) & 7) - 6 - 2 * yb
        local = ex * 48 + ey * 8 + (site & 7)
        local = jnp.where(present, local, -1)
        spread = nn(local.astype(F32).astype(BF16), slot_pick_ref[...])
        yield
        index = jnp.sum(spread * atom_mask_ref[...].astype(F32), axis=0, keepdims=True)
        hot[slot, 0:240, :] = jnp.where(hot_rows == index, 1.0, 0.0).astype(BF16)
        hot[slot, 240:256, :] = atom_mask_ref[...]
        yield
        parts = [far_tab[pl.ds(pl.multiple_of(base + 96 * i, 16), 48), :] for i in range(5)]
        parts.append(own_tab[pl.ds(pl.multiple_of(base + 208, 16), 16), :])
        table = jnp.concatenate(parts, axis=0)
        picked = tn(table, hot[slot])
        yield
        gat[slot] = picked

    def network(block, slot):
        mask = atom_mask_ref[...].astype(F32)
        wide_mask = atom_wide_ref[...].astype(F32)

        def prepare(k):
            species_row = lax.broadcasted_iota(jnp.int32, (8, PAIRS), 0).astype(F32)
            hot_own = jnp.where(species_row == feat[slot + k, 17:18, :], 1.0, 0.0)
            hot_far = jnp.where(species_row == feat[slot + k, 18:19, :], 1.0, 0.0)
            nil = jnp.zeros((8, PAIRS), F32)
            x0[k] = jnp.concatenate([feat[slot + k, 0:8, :], hot_own, hot_far, nil], axis=0).astype(BF16)
            for i in range(8):
                hbd[k, 16 * i : 16 * i + 16, :] = (feat[slot + k, 8 + i : 9 + i, :] * mask).astype(BF16)
            hbd[k, 128:144, :] = atom_mask_ref[...]
            yield

        def env(k, cols):
            return feat[slot + k, 16:17, cols]

        sums = {}

        def gather_sum(key, part):
            sums[key] = sums[key] + part if key in sums else part

        def stage_a(k, cols):
            half = nn(embed_t[:, 0:32], x0[k, :, cols])
            yield
            value, slope = swish(half)
            ss[k, 0, :, cols] = value.astype(BF16)
            dd[k, 0, :, cols] = (slope * (0.5 * env(k, cols))).astype(BF16)
            latent = value * env(k, cols)
            packed = latent.astype(BF16)
            j0[k, 0:128, cols] = packed
            we = nn(we_t[...], packed)
            yield
            w_s[k, :, cols] = we[0:32]
            coeff = we[32:64].astype(BF16)
            cat[k, 224:256, cols] = coeff
            gather_sum(("e0", k), nt(coeff, hbd[k, :, cols]))
            yield

        def between_a(k):
            environ = sums["e0", k] * NORM
            sums["e0", k] = environ
            eb[k, 0, :, 0:144] = (jnp.concatenate([environ] * 3, axis=0) * degree_mask_ref[...]).astype(BF16)
            e0t[k, :, 0:32] = environ.T.astype(BF16)
            yield
            spread = nn(e0t[k, :, 0:32], chan_wide_ref[...])
            yield
            for i in range(9):
                e0x[k, i : i + 1, :] = jnp.sum(
                    spread[16 * i : 16 * i + 16, :] * wide_mask, axis=0, keepdims=True
                )

        def stage_b(k, cols):
            q = nn(eb[k, 0, :, 0:144], hbd[k, :, cols])
            yield
            q_s[k, :, cols] = q
            w3 = jnp.concatenate([w_s[k, :, cols]] * 3, axis=0)
            scal = (q * w3).astype(BF16)
            j0[k, 128:224, cols] = scal
            half = nn(l1_t[:, 0:224], j0[k, :, cols])
            mixed = nn(mix_t[:, 0:32], scal[0:32])
            yield
            a_s[k, :, cols] = mixed
            value, slope = swish(half)
            ss[k, 1, :, cols] = value.astype(BF16)
            dd[k, 1, :, cols] = (slope * (0.5 * env(k, cols))).astype(BF16)
            latent = j0[k, 0:128, cols].astype(F32) + value * env(k, cols)
            packed = latent.astype(BF16)
            j1[k, 0:128, cols] = packed
            coeff = nn(e1_t[...], packed)
            yield
            coeff = coeff.astype(BF16)
            cat[k, 192:224, cols] = coeff
            gather_sum(("e1", k), nt(coeff, hbd[k, :, cols]))
            yield

        def spread_w(k, half):
            w = w_s[k, :, halves[half]]
            m8 = mask[8 * half : 8 * half + 8, halves[half]]
            return jnp.concatenate([w * m8[p : p + 1, :] for p in range(8)], axis=0).astype(BF16)

        def stage_c(k):
            environ = sums["e1", k] * NORM
            sums["e1", k] = environ
            eb[k, 1, :, 0:144] = (jnp.concatenate([environ] * 3, axis=0) * degree_mask_ref[...]).astype(BF16)
            e1r[k, :, 0:16] = jnp.concatenate(
                [environ[:, 16 * i : 16 * i + 16] for i in range(9)], axis=0
            ).astype(BF16)
            yield
            for i in range(9):
                e1x[k, 32 * i : 32 * i + 32, :] = nn(e1r[k, 32 * i : 32 * i + 32, 0:16], atom_wide_ref[...])
            for half in range(2):
                ww[k, half] = spread_w(k, half)
            yield
            for d in range(3):
                total = None
                for i in range(9):
                    if DEGREE_OF[i] == d:
                        part = e1x[k, 32 * i : 32 * i + 32, :] * e0x[k, i : i + 1, :]
                        total = part if total is None else total + part
                rows = slice(32 * d, 32 * d + 32)
                bmat[k, rows, :] = (total * mix_wide[rows, :]).astype(BF16)
            yield
            for half in range(2):
                r_s[k, :, halves[half]] = nn(bmat[k, :, wides[half]], ww[k, half])
            yield

        def stage_d(k, cols):
            q = nn(eb[k, 1, :, 0:144], hbd[k, :, cols])
            yield
            a = a_s[k, :, cols]
            q1_s[k, :, cols] = q
            j1[k, 128:224, cols] = (a * q + r_s[k, :, cols]).astype(BF16)
            half = nn(l2_t[:, 0:224], j1[k, :, cols])
            yield
            value, slope = swish(half)
            ss[k, 2, :, cols] = value.astype(BF16)
            dd[k, 2, :, cols] = (slope * (0.5 * env(k, cols))).astype(BF16)
            latent = j1[k, 0:128, cols].astype(F32) + value * env(k, cols)
            half = nn(out_t[...], latent.astype(BF16))
            yield
            hidden, slope = swish(half)
            weighted = eighth(hidden * vec_b[...])
            t_s[k, :, cols] = weighted
            dz = (slope * vec_b[...] * (0.5 * env(k, cols))).astype(BF16)
            dzs[k, 0:128, cols] = dz
            dl = nn(out_ref[...], dz)
            pair_energy[k, :, cols] = jnp.sum(weighted, axis=0, keepdims=True) * env(k, cols)
            yield
            t_s[k, :, cols] = t_s[k, :, cols] + eighth(dl * ss[k, 2, :, cols].astype(F32))
            dz = (dl * dd[k, 2, :, cols].astype(F32)).astype(BF16)
            dzs[k, 128:256, cols] = dz
            dscal = nn(latent_ref[1, 128:224, :], dz)
            yield
            ds_b[k, :, cols] = dscal.astype(BF16)
            dmix = nn(mix_all[:, 0:96], (dscal * q1_s[k, :, cols]).astype(BF16))
            dq = (dscal * a_s[k, :, cols]).astype(BF16)
            cat[k, 0:96, cols] = dq
            gather_sum(("d1", k), nt(dq, hbd[k, :, cols]))
            yield
            small[k, :, cols] = dmix

        def stage_e(k):
            row = pair_energy[k]
            high, middle, low = pieces(row, 3)
            fill = jnp.zeros((5, PAIRS), F32)
            total = nt(jnp.concatenate([high, middle, low, fill], axis=0).astype(BF16), atom_mask_ref[...])
            energy_ref[pl.ds(place(block + k)[3], 1), :] = total[0:1] + (total[1:2] + total[2:3])
            for half in range(2):
                db[k, :, wides[half]] = nt(ds_b[k, :, halves[half]], ww[k, half])
                back = tn(bmat[k, :, wides[half]], ds_b[k, :, halves[half]])
                m8 = mask[8 * half : 8 * half + 8, halves[half]]
                total = back[0:32] * m8[0:1]
                for p in range(1, 8):
                    total = total + back[32 * p : 32 * p + 32] * m8[p : p + 1]
                dwr[k, :, halves[half]] = total
            yield
            inner = []
            for i in range(9):
                rows = slice(32 * DEGREE_OF[i], 32 * DEGREE_OF[i] + 32)
                piece = db[k, rows, :] * mix_wide[rows, :]
                outer[k, 32 * i : 32 * i + 32, :] = (piece * e0x[k, i : i + 1, :]).astype(BF16)
                inner.append(jnp.sum(piece * e1x[k, 32 * i : 32 * i + 32, :], axis=0, keepdims=True))
            yield
            side = nt(outer[k], atom_wide_ref[...])
            de0t = nt(jnp.concatenate([r * wide_mask for r in inner], axis=0).astype(BF16), chan_wide_ref[...])
            yield
            de = sums["d1", k] * degree_mask_ref[...]
            de = de[0:32] + de[32:64] + de[64:96]
            de = de + jnp.concatenate([side[32 * i : 32 * i + 32, :] for i in range(9)], axis=1)
            de = de * NORM
            sums["d1", k] = de
            de_b[k, 1, :, 0:144] = de.astype(BF16)
            sums["side0", k] = de0t.T

        def stage_f(k, cols):
            dcoeff = nn(de_b[k, 1, :, 0:144], hbd[k, :, cols])
            yield
            dzs[k, 256:288, cols] = dcoeff.astype(BF16)
            dl = nn(back_w[:, 0:288], dzs[k, 0:288, cols])
            yield
            t_s[k, :, cols] = t_s[k, :, cols] + eighth(dl * ss[k, 1, :, cols].astype(F32))
            dz = (dl * dd[k, 1, :, cols].astype(F32)).astype(BF16)
            dzs[k, 288:416, cols] = dz
            dscal = nn(latent_ref[0, 128:224, :], dz)
            yield
            dscal = [dscal[0:32] + small[k, :, cols], dscal[32:64], dscal[64:96]]
            w = w_s[k, :, cols]
            dw = dwr[k, :, cols]
            for d in range(3):
                cat[k, 96 + 32 * d : 128 + 32 * d, cols] = (dscal[d] * w).astype(BF16)
                dw = dw + dscal[d] * q_s[k, 32 * d : 32 * d + 32, cols]
            dzs[k, 416:448, cols] = dw.astype(BF16)
            gather_sum(("d0", k), nt(cat[k, 96:192, cols], hbd[k, :, cols]))
            yield

        def between_f(k):
            de = sums["d0", k] * degree_mask_ref[...]
            de = (de[0:32] + de[32:64] + de[64:96] + sums["side0", k]) * NORM
            de_b[k, 0, :, 0:144] = de.astype(BF16)
            yield
            e0, e1, d1 = sums["e0", k], sums["e1", k], sums["d1", k]
            tall = []
            for e in (e1, e0):
                three = jnp.concatenate([e[:, 0:128]] * 3, axis=0)
                tall.append(three * degree_mask_ref[:, 0:128])
            tall += [d1[:, 0:128], de[:, 0:128]]
            left[k] = jnp.concatenate(tall, axis=0).T.astype(BF16)
            yield

        def stage_h(k, cols):
            dcoeff = nn(de_b[k, 0, :, 0:144], hbd[k, :, cols])
            dhbd = nn(left[k], cat[k, :, cols])
            yield
            dzs[k, 448:480, cols] = dcoeff.astype(BF16)
            dl = nn(back_w[:, 0:480], dzs[k, 0:480, cols])
            for i in range(8):
                dfeat[slot + k, 8 + i : 9 + i, cols] = jnp.sum(
                    dhbd[16 * i : 16 * i + 16, :] * mask[:, cols], axis=0, keepdims=True
                )
            yield
            dz = (dl * dd[k, 0, :, cols].astype(F32)).astype(BF16)
            dradial = nn(embed_ref[...], dz)
            dfeat[slot + k, 16:17, cols] = jnp.sum(
                t_s[k, :, cols] + eighth(dl * ss[k, 0, :, cols].astype(F32)), axis=0, keepdims=True
            )
            yield
            dfeat[slot + k, 0:8, cols] = dradial[0:8]

        members = range(UNIT)
        for stage, tiled in (
            (prepare, False),
            (stage_a, True),
            (between_a, False),
            (stage_b, True),
            (stage_c, False),
            (stage_d, True),
            (stage_e, False),
            (stage_f, True),
            (between_f, False),
            (stage_h, True),
        ):
            if tiled:
                together([stage(k, cols) for k in members for cols in tiles])
            else:
                together([stage(k) for k in members])

    def scatter(block, slot):
        pulled = nt(hot[slot], dfeat[slot, 0:16, :].astype(BF16))
        yield
        _, base, _, _ = place(block)
        for i in range(5):
            rows = pl.ds(pl.multiple_of(base + 96 * i, 16), 48)
            ftab[rows, :] = ftab[rows, :] - pulled[48 * i : 48 * i + 48, :]
        rows = pl.ds(pl.multiple_of(base + 208, 16), 16)
        ftab[rows, :] = ftab[rows, :] + pulled[240:256, :]

    blocks = own_blocks + lent_blocks

    def chunk_step(chunk, carry):
        first = chunk * CHUNK

        def rows_of(ref):
            return lambda f: jnp.concatenate([ref[b, f : f + 1, :] for b in range(CHUNK)], axis=0)

        def rows_to(ref):
            def put(f, value):
                for b in range(CHUNK):
                    ref[b, f : f + 1, :] = value[b : b + 1, :]

            return put

        together([fetch(first + k, k) for k in range(UNIT)])
        geometry(rows_of(gat), rows_to(feat), geo)
        network(first, 0)
        geometry_back(rows_of(dfeat), rows_to(dfeat), geo)
        together([scatter(first + k, k) for k in range(UNIT)])
        return carry

    lax.fori_loop(0, (blocks + CHUNK - 1) // CHUNK, chunk_step, 0)

    def leave(force_ref, per_plane, first_y, planes=12, first_row=0):
        rows = jnp.concatenate(
            [
                ftab[first_row + p * 96 + first_y * LZ : first_row + p * 96 + first_y * LZ + per_plane, :]
                for p in range(planes)
            ],
            axis=0,
        )
        turned_rows = rows.T
        force_ref[...] = turned_rows[0:3] + turned_rows[3:6]

    leave(fmid_ref, 64, 2)
    leave(flow_ref, 16, 0)
    leave(fhigh_ref, 16, 10)
    leave(flent_ref, 96, 0, 6, 1152)


def pair_call(blocks, mid, low, high, neighbors, used, lent, lent_sites, params):
    embed, first, env, latent, mix, out, vector = params
    sites = neighbors.shape[0]
    atom_mask, slot_pick, atom_wide, chan_wide, degree_mask = constants()
    consts = [
        jnp.asarray(atom_mask, BF16),
        jnp.asarray(slot_pick, BF16),
        jnp.asarray(atom_wide, BF16),
        jnp.asarray(chan_wide, BF16),
        jnp.asarray(degree_mask, F32),
    ]
    vm = pl.BlockSpec(memory_space=pltpu.VMEM)
    sm = pl.BlockSpec(memory_space=pltpu.SMEM)
    scratch = [
        ((608, SLOTS), jnp.int32),
        ((1728, 16), BF16),
        ((1728, 16), BF16),
        ((1728, 16), F32),
        ((128, 128), BF16),
        ((64, 128), BF16),
        ((128, 256), BF16),
        ((128, 256), BF16),
        ((32, 128), BF16),
        ((128, 128), BF16),
        ((96, 128), BF16),
        ((32, 128), BF16),
        ((96, 512), F32),
        ((128, TILE), F32),
        ((CHUNK, 256, PAIRS), BF16),
        ((CHUNK, 16, PAIRS), F32),
        ((CHUNK, 24, PAIRS), F32),
        ((CHUNK, 24, PAIRS), F32),
        ((14, CHUNK, PAIRS), F32),
        ((UNIT, 32, PAIRS), BF16),
        ((UNIT, 144, PAIRS), BF16),
        ((UNIT, 3, 128, PAIRS), BF16),
        ((UNIT, 3, 128, PAIRS), BF16),
        ((UNIT, 224, PAIRS), BF16),
        ((UNIT, 224, PAIRS), BF16),
        ((UNIT, 32, PAIRS), F32),
        ((UNIT, 256, PAIRS), BF16),
        ((UNIT, 96, PAIRS), F32),
        ((UNIT, 96, PAIRS), F32),
        ((UNIT, 96, PAIRS), F32),
        ((UNIT, 96, PAIRS), F32),
        ((UNIT, 96, PAIRS), BF16),
        ((UNIT, 8, PAIRS), F32),
        ((UNIT, 32, PAIRS), F32),
        ((UNIT, 32, PAIRS), F32),
        ((UNIT, 16, 512), F32),
        ((UNIT, 288, 512), F32),
        ((UNIT, 96, 512), BF16),
        ((UNIT, 2, 96, 256), BF16),
        ((UNIT, 144, 128), BF16),
        ((UNIT, 288, 128), BF16),
        ((UNIT, 2, 256, 384), BF16),
        ((UNIT, 1, PAIRS), F32),
        ((UNIT, 96, 512), F32),
        ((UNIT, 288, 512), BF16),
        ((UNIT, 2, 32, 256), BF16),
        ((UNIT, 128, 256), BF16),
        ((UNIT, 480, PAIRS), BF16),
        ((128, 512), BF16),
    ]
    return pl.pallas_call(
        pair_kernel,
        out_shape=[
            jax.ShapeDtypeStruct((sites // GROUP + 8, GROUP), F32),
            jax.ShapeDtypeStruct((3, 768), F32),
            jax.ShapeDtypeStruct((3, 192), F32),
            jax.ShapeDtypeStruct((3, 192), F32),
            jax.ShapeDtypeStruct((3, 576), F32),
        ],
        in_specs=[sm] + [vm] * 19,
        out_specs=[vm] * 5,
        scratch_shapes=[pltpu.VMEM(shape, dtype) for shape, dtype in scratch],
        compiler_params=pltpu.CompilerParams(vmem_limit_bytes=48 * 1024 * 1024),
        name="pair_terms",
    )(blocks, mid, low, high, neighbors, used, lent, lent_sites, embed, first, env, latent, mix[0], out, vector.reshape(1, -1), *consts)


def route_kernel(me_ref, shares_ref, boxes_ref, forward_ref, lender_ref, blocks_ref):
    count = shares_ref.shape[0]
    me = me_ref[0]
    down = lax.broadcasted_iota(jnp.int32, (count, count), 0)
    right = lax.broadcasted_iota(jnp.int32, (count, count), 1)
    need = shares_ref[:, 3 * SHARE : 3 * SHARE + 1]
    need_down = jnp.broadcast_to(need, (count, count))
    need_right = jnp.sum(jnp.where(down == right, need_down, 0.0), axis=0, keepdims=True)
    need_right = jnp.broadcast_to(need_right, (count, count))
    full_down = need_down > LIGHT_BLOCKS + 0.5
    full_right = need_right > LIGHT_BLOCKS + 0.5
    rank_down = jnp.sum(jnp.where(full_right & (right < down), 1.0, 0.0), axis=1, keepdims=True)
    rank_down = jnp.broadcast_to(rank_down, (count, count))
    rank_right = jnp.sum(jnp.where(full_down & (down < right), 1.0, 0.0), axis=0, keepdims=True)
    rank_right = jnp.broadcast_to(rank_right, (count, count))
    light_down = jnp.where(full_down, -1.0, down.astype(F32) - rank_down)
    light_right = jnp.where(full_right, -1.0, right.astype(F32) - rank_right)
    lends_right = jnp.where(full_right, 3.0 * rank_right, 1000.0)
    lends_down = jnp.where(full_down, 3.0 * rank_down, 1000.0)
    total = jnp.zeros((count, SHARE), F32)
    boxes = jnp.zeros((count, BOX), F32)
    lender = jnp.zeros((count, 1), F32)
    parts = jnp.zeros((count, 1), F32)
    for j in range(3):
        choice = jnp.where(light_down == lends_right + j, 1.0, 0.0)
        names = shares_ref[:, j * SHARE : (j + 1) * SHARE]
        high, low = pieces(names, 2)
        choice_b = choice.astype(BF16)
        total = total + (nn(choice_b, high.astype(BF16)) + nn(choice_b, low.astype(BF16)))
        mine = jnp.sum(jnp.where(right == me, choice, 0.0), axis=1, keepdims=True)
        boxes = boxes + mine * boxes_ref[j : j + 1, :]
        taken = jnp.where((light_right == lends_down + j) & (right == me), 1.0, 0.0)
        taken = jnp.sum(taken, axis=1, keepdims=True)
        lender = lender + taken
        parts = parts + j * taken
    forward_ref[:, 0:SHARE] = total
    forward_ref[:, SHARE : SHARE + BOX] = boxes
    lender_ref[...] = lender
    here = lax.broadcasted_iota(jnp.int32, (count, 1), 0) == me
    own_need = jnp.sum(jnp.where(here, need, 0.0)).astype(jnp.int32)
    lent_need = jnp.sum(lender * need).astype(jnp.int32)
    part = jnp.sum(parts).astype(jnp.int32)
    first = KEPT + LENT * part
    blocks_ref[0] = jnp.where(own_need > LIGHT_BLOCKS, jnp.minimum(own_need, KEPT), own_need)
    blocks_ref[1] = jnp.minimum(jnp.maximum(lent_need - first, 0), LENT)
    blocks_ref[2] = first
    blocks_ref[3] = part


def route_call(me, shares, boxes):
    count = shares.shape[0]
    vm = pl.BlockSpec(memory_space=pltpu.VMEM)
    sm = pl.BlockSpec(memory_space=pltpu.SMEM)
    return pl.pallas_call(
        route_kernel,
        out_shape=[
            jax.ShapeDtypeStruct((count, SHARE + BOX), F32),
            jax.ShapeDtypeStruct((count, 1), F32),
            jax.ShapeDtypeStruct((4,), jnp.int32),
        ],
        in_specs=[sm, vm, vm],
        out_specs=[vm, vm, sm],
        name="route",
    )(me, shares, boxes)


def ring(axis, by):
    count = lax.axis_size(axis)
    return [(i, (i + by) % count) for i in range(count)]


def on_device(positions, species, neighbors, slot_used, *params):
    sites = species.shape[-1]
    count = lax.axis_size("yz")
    me = lax.axis_index("yz")
    near = neighbors.reshape(sites, SLOTS)
    used = slot_used.reshape(sites, SLOTS)
    own = jnp.concatenate(
        [positions.reshape(3, sites), species.reshape(1, sites).astype(F32)], axis=0
    )
    up_x, down_x = ring("gx", 1), ring("gx", -1)
    up_y, down_y = ring("yz", 1), ring("yz", -1)
    before = lax.ppermute(own[:, 384:512], "gx", up_x)
    after = lax.ppermute(own[:, 0:128], "gx", down_x)
    mid = jnp.concatenate([before, own, after], axis=1)
    planes = mid.reshape(4, 12, 64)
    low = lax.ppermute(planes[:, :, 48:64].reshape(4, 192), "yz", up_y)
    high = lax.ppermute(planes[:, :, 0:16].reshape(4, 192), "yz", down_y)
    filled = jnp.max(jnp.where(used > 0, lax.broadcasted_iota(jnp.int32, used.shape, 0) + 1, 0))
    need = (filled + GROUP - 1) // GROUP

    last = slice(KEPT * GROUP, sites)
    codes = jnp.where(used[last] > 0, near[last], -1).astype(F32).reshape(3, count, SHARE)
    shares = codes.transpose(1, 0, 2).reshape(count, 3 * SHARE)
    shares = jnp.concatenate([shares, jnp.full((count, 1), need, jnp.int32).astype(F32)], axis=1)
    shares = lax.all_to_all(shares, "yz", 0, 0, tiled=True)
    box = jnp.concatenate([low.reshape(4, 12, 16), planes, high.reshape(4, 12, 16)], axis=2)
    firsts = [KEPT + LENT * j for j in range(3)]
    boxes = jnp.concatenate([box[:, f // 4 : f // 4 + 6].reshape(1, BOX) for f in firsts], axis=0)
    forward, lender, blocks = route_call(me.astype(jnp.int32).reshape(1), shares, boxes)
    lent = lax.all_to_all(forward, "yz", 0, 0, tiled=True)
    lent_codes = lent[:, 0:SHARE].reshape(2 * SLOTS, SLOTS)
    lent_sites = jnp.sum(lent[:, SHARE:] * lender, axis=0).reshape(4, 576)
    part = blocks[3]

    energy, fmid, flow, fhigh, flent = pair_call(
        blocks, mid, low, high, near, used, lent_codes, lent_sites, params
    )

    lent_force = flent.reshape(3, 6, 96)
    wide = sum(
        jnp.where(part == j, jnp.pad(lent_force, ((0, 0), (f // 4, 6 - f // 4), (0, 0))), 0.0)
        for j, f in enumerate(firsts)
    )

    def to_low(edge):
        return jnp.pad(edge, ((0, 0), (0, 0), (48, 0))).reshape(1, -1)

    def to_high(edge):
        return jnp.pad(edge, ((0, 0), (0, 0), (0, 48))).reshape(1, -1)

    device = jnp.arange(count, dtype=jnp.int32)
    home = lender
    home_low = jnp.roll(lender, -1, axis=0)
    home_high = jnp.roll(lender, 1, axis=0)
    me_low = (device == (me + count - 1) % count).astype(F32)[:, None]
    me_high = (device == (me + 1) % count).astype(F32)[:, None]
    sent = (
        home * wide[:, :, 16:80].reshape(1, -1)
        + home_low * to_low(wide[:, :, 0:16])
        + home_high * to_high(wide[:, :, 80:96])
        + me_low * to_low(flow.reshape(3, 12, 16))
        + me_high * to_high(fhigh.reshape(3, 12, 16))
    )
    lent_energy = energy[32:38].reshape(1, 96)
    parts = [jnp.where(part == j, home * lent_energy, 0.0) for j in range(3)]
    got = lax.all_to_all(jnp.concatenate([sent] + parts, axis=1), "yz", 0, 0, tiled=True)
    got = jnp.sum(got, axis=0)
    column = fmid + got[0:2304].reshape(3, 768)
    own_energy = energy[0:32].reshape(sites) + jnp.pad(got[2304:2592], (KEPT * GROUP, 0))
    from_after = lax.ppermute(column[:, 0:128], "gx", down_x)
    from_before = lax.ppermute(column[:, 640:768], "gx", up_x)
    gap = jnp.zeros((3, 256), F32)
    forces = column[:, 128:640] + jnp.concatenate([from_before, gap, from_after], axis=1)
    return (own_energy.reshape(1, 1, sites), forces.reshape(3, 1, 1, sites))


def solution(mesh):
    in_specs = (
        P(None, "gx", "yz", None),
        P("gx", "yz", None),
        P("gx", "yz", None, None),
        P("gx", "yz", None, None),
        P(),
        P(),
        P(),
        P(),
        P(),
        P(),
        P(),
    )
    out_specs = (P("gx", "yz", None), P(None, "gx", "yz", None))
    return jax.shard_map(
        on_device, mesh=mesh, in_specs=in_specs, out_specs=out_specs, check_vma=False
    )
```

```python
import functools
import math

import jax
import jax.numpy as jnp
import numpy as np
from jax import lax
from jax.experimental import pallas as pl
from jax.experimental.pallas import tpu as pltpu
from jax.sharding import PartitionSpec as P

F32 = jnp.float32
BF16 = jnp.bfloat16
LZ = 8
NRAD = 8
CH = 32
SLOTS = 48
GROUP = 16
PAIRS = GROUP * SLOTS
UNIT = 7
CHUNK = UNIT
TILE = 256
KEPT = 14
LENT = 6
LIGHT_BLOCKS = 8
SHARE = 144
BOX = 2304
NORM = 1.0 / math.sqrt(SLOTS)
RADIAL_GAIN = math.sqrt(2.0 / 5.0)
DEGREES = ((0,), (1, 2, 3), (4, 5, 6, 7, 8))
ORDER = (1, 2, 3, 4, 5, 6, 7, 8, 0)
DEGREE_OF = tuple(next(d for d in range(3) if m in DEGREES[d]) for m in ORDER)


def nn(a, b):
    return jnp.dot(a, b, preferred_element_type=F32)


def nt(a, b):
    return lax.dot_general(a, b, (((1,), (1,)), ((), ())), preferred_element_type=F32)


def tn(a, b):
    return lax.dot_general(a, b, (((0,), (0,)), ((), ())), preferred_element_type=F32)


def eighth(value):
    return jnp.sum(value.reshape(value.shape[0] // 8, 8, value.shape[1]), axis=0)


def pieces(value, count):
    out = []
    for _ in range(count):
        part = value.astype(BF16).astype(F32)
        out.append(part)
        value = value - part
    return out


def constants():
    lane = np.arange(PAIRS)
    atom_mask = (lane[None, :] // SLOTS == np.arange(GROUP)[:, None]).astype(np.float32)
    slot_pick = (lane[None, :] % SLOTS == np.arange(SLOTS)[:, None]).astype(np.float32)
    wide = np.arange(GROUP * CH)
    atom_wide = (wide[None, :] // CH == np.arange(GROUP)[:, None]).astype(np.float32)
    chan_wide = (wide[None, :] % CH == np.arange(CH)[:, None]).astype(np.float32)
    degree_mask = np.zeros((96, 144), np.float32)
    for i, d in enumerate(DEGREE_OF):
        degree_mask[d * 32 : d * 32 + 32, i * 16 : i * 16 + 16] = 1.0
    return atom_mask, slot_pick, atom_wide, chan_wide, degree_mask


def geometry(get, put, geo):
    used = get(14) > 0.5
    one = jnp.ones((CHUNK, PAIRS), F32)
    nil = jnp.zeros((CHUNK, PAIRS), F32)
    vx = jnp.where(used, get(0) + (get(3) + get(6)) + get(9), one)
    vy = jnp.where(used, get(1) + (get(4) + get(7)) + get(10), nil)
    step_z = get(11)
    step_z = jnp.where(step_z >= 4.0, step_z - 8.0, jnp.where(step_z < -4.0, step_z + 8.0, step_z))
    vz = jnp.where(used, get(2) + (get(5) + get(8)) + step_z, nil)
    keep = jnp.where(used, one, nil)
    square = vx * vx + vy * vy + vz * vz
    inv = lax.rsqrt(square)
    inv = inv * (1.5 - 0.5 * square * inv * inv)
    length = square * inv
    ux, uy, uz = vx * inv, vy * inv, vz * inv
    t = length * 0.2
    t2 = t * t
    t5 = t2 * t2 * t
    t6 = t5 * t
    envelope = (1.0 - 28.0 * t6 + 48.0 * t6 * t - 21.0 * t6 * t2) * keep
    slope = t5 * (-168.0 + 336.0 * t - 168.0 * t2) * (0.2 * keep)
    y = length * (math.pi / 5.0) - (math.pi / 2.0)
    y2 = y * y
    sine = 1.0 + y2 * (
        -1.0 / 2
        + y2 * (1.0 / 24 + y2 * (-1.0 / 720 + y2 * (1.0 / 40320 + y2 * (-1.0 / 3628800 + y2 * (1.0 / 479001600)))))
    )
    cosine = -y * (
        1.0
        + y2
        * (-1.0 / 6 + y2 * (1.0 / 120 + y2 * (-1.0 / 5040 + y2 * (1.0 / 362880 + y2 * (-1.0 / 39916800)))))
    )
    twice = 2.0 * cosine
    sines, cosines = [nil, sine], [one, cosine]
    for _ in range(NRAD - 1):
        sines.append(twice * sines[-1] - sines[-2])
        cosines.append(twice * cosines[-1] - cosines[-2])
    scale = RADIAL_GAIN * inv
    for n in range(1, NRAD + 1):
        radial = scale * sines[n]
        put(n - 1, radial)
        geo[n - 1] = ((n * math.pi / 5.0) * scale) * cosines[n] - radial * inv
    r3, r5, r15 = math.sqrt(3.0), math.sqrt(5.0), math.sqrt(15.0)
    harmonic = [
        r3 * ux,
        r3 * uy,
        r3 * uz,
        r15 * ux * uy,
        r15 * uy * uz,
        0.5 * r5 * (3.0 * uz * uz - 1.0),
        r15 * ux * uz,
        0.5 * r15 * (ux * ux - uy * uy),
    ]
    for i, value in enumerate(harmonic):
        put(8 + i, value)
    put(16, envelope)
    put(17, get(13))
    put(18, get(12))
    geo[8] = slope
    geo[9] = ux
    geo[10] = uy
    geo[11] = uz
    geo[12] = inv
    geo[13] = keep


def geometry_back(get, put, geo):
    slope, ux, uy, uz, inv, keep = (geo[8 + i] for i in range(6))
    along = get(16) * slope
    for n in range(NRAD):
        along = along + get(n) * geo[n]
    g1, g2, g3, g4, g5, g6, g7, g8 = (get(8 + i) for i in range(8))
    r3, r5, r15 = math.sqrt(3.0), math.sqrt(5.0), math.sqrt(15.0)
    ax = r3 * g1 + r15 * (uy * g4 + uz * g7 + ux * g8)
    ay = r3 * g2 + r15 * (ux * g4 + uz * g5 - uy * g8)
    az = r3 * g3 + r15 * (uy * g5 + ux * g7) + (3.0 * r5) * uz * g6
    radial_part = along - (ax * ux + ay * uy + az * uz) * inv
    for i, (a, u) in enumerate(((ax, ux), (ay, uy), (az, uz))):
        high, low = pieces(jnp.where(keep > 0.5, radial_part * u + a * inv, 0.0), 2)
        put(i, high)
        put(3 + i, low)


def swish(half):
    wide = 1.0 + jnp.tanh(half)
    value = half * wide
    return value, wide + value * (2.0 - wide)


def together(streams):
    while streams:
        left = []
        for stream in streams:
            try:
                next(stream)
                left.append(stream)
            except StopIteration:
                pass
        streams = left


def pair_kernel(
    blocks_ref,
    mid_ref,
    low_ref,
    high_ref,
    neighbors_ref,
    used_ref,
    lent_ref,
    lent_sites_ref,
    embed_ref,
    first_ref,
    env_ref,
    latent_ref,
    mix_ref,
    out_ref,
    vector_ref,
    atom_mask_ref,
    slot_pick_ref,
    atom_wide_ref,
    chan_wide_ref,
    degree_mask_ref,
    energy_ref,
    fmid_ref,
    flow_ref,
    fhigh_ref,
    flent_ref,
    codes,
    far_tab,
    own_tab,
    ftab,
    embed_t,
    we_t,
    l1_t,
    l2_t,
    e1_t,
    out_t,
    mix_t,
    mix_all,
    mix_wide,
    vec_b,
    hot,
    gat,
    feat,
    dfeat,
    geo,
    x0,
    hbd,
    dd,
    ss,
    j0,
    j1,
    w_s,
    cat,
    q_s,
    q1_s,
    a_s,
    r_s,
    ds_b,
    t_s,
    small,
    dwr,
    e0x,
    e1x,
    bmat,
    eb,
    e0t,
    e1r,
    ww,
    pair_energy,
    db,
    outer,
    de_b,
    left,
    dzs,
    back_w,
):
    def turned(value):
        return value.astype(F32).T

    for ref in (embed_t, l1_t, l2_t, mix_t, mix_all, back_w, eb, e0t, e1r, de_b):
        ref[...] = jnp.zeros_like(ref)
    embed_t[:, 0:24] = (turned(embed_ref[...]) * 0.5).astype(BF16)
    we_t[0:32, :] = turned(first_ref[...]).astype(BF16)
    we_t[32:64, :] = turned(env_ref[0]).astype(BF16)
    e1_t[...] = turned(env_ref[1]).astype(BF16)
    l1_t[:, 0:224] = (turned(latent_ref[0]) * 0.5).astype(BF16)
    l2_t[:, 0:224] = (turned(latent_ref[1]) * 0.5).astype(BF16)
    out_t[...] = (turned(out_ref[...]) * 0.5).astype(BF16)
    back_w[:, 0:480] = jnp.concatenate(
        [out_ref[...], latent_ref[1, 0:128], env_ref[1], latent_ref[0, 0:128], first_ref[...], env_ref[0]],
        axis=1,
    )
    mix_all[:, 0:96] = jnp.concatenate([mix_ref[d] for d in range(3)], axis=1)
    for d in range(3):
        mix_t[32 * d : 32 * d + 32, 0:32] = turned(mix_ref[d]).astype(BF16)
    mix_wide[...] = nn(mix_t[:, 0:32], chan_wide_ref[...])
    vec_b[...] = jnp.broadcast_to(vector_ref[...].T, (128, TILE))

    def enter(values_ref, per_plane, first_y, planes=12, first_row=0):
        count = values_ref.shape[1]
        lane = lax.broadcasted_iota(jnp.int32, (1, count), 1)
        plane = lane // per_plane
        rest = lane - plane * per_plane
        column = rest // LZ
        lattice = [plane.astype(F32), (column + first_y).astype(F32), (rest - column * LZ).astype(F32)]
        xyz = values_ref[0:3, :]
        kind = values_ref[3:4, :]
        one = jnp.ones((1, count), F32)
        nil = jnp.zeros((1, count), F32)
        places = jnp.concatenate(pieces(xyz, 3) + lattice, axis=0)
        far = jnp.concatenate([places, kind, nil, one, nil], axis=0).T.astype(BF16)
        own = jnp.concatenate([-places, nil, kind, nil, nil], axis=0).T.astype(BF16)
        for p in range(planes):
            start = first_row + p * 96 + first_y * LZ
            far_tab[start : start + per_plane, :] = far[p * per_plane : (p + 1) * per_plane, :]
            own_tab[start : start + per_plane, :] = own[p * per_plane : (p + 1) * per_plane, :]

    enter(mid_ref, 64, 2)
    enter(low_ref, 16, 0)
    enter(high_ref, 16, 10)
    enter(lent_sites_ref, 96, 0, 6, 1152)
    codes[0:512, :] = jnp.where(used_ref[...] > 0, neighbors_ref[...], -1)
    codes[512:608, :] = lent_ref[...].astype(jnp.int32)
    ftab[...] = jnp.zeros_like(ftab)
    energy_ref[...] = jnp.zeros_like(energy_ref)
    gat[...] = jnp.zeros_like(gat)
    dfeat[...] = jnp.zeros_like(dfeat)
    hot_rows = lax.broadcasted_iota(jnp.int32, (240, PAIRS), 0).astype(F32)
    tiles = [slice(TILE * j, TILE * j + TILE) for j in range(PAIRS // TILE)]
    halves = [slice(0, 384), slice(384, 768)]
    wides = [slice(0, 256), slice(256, 512)]

    own_blocks, lent_blocks, lent_first = blocks_ref[0], blocks_ref[1], blocks_ref[2]

    def place(block):
        step = block - own_blocks
        lent = step >= 0
        step = jnp.minimum(step, LENT - 1)
        home = jnp.where(lent, lent_first + step, block)
        plane = home // 4 - jnp.where(lent, lent_first // 4 - 12, 0)
        base = plane * 96 + (home % 4) * 16
        row = jnp.where(block < own_blocks + lent_blocks, jnp.where(lent, 32 + step, home), 39)
        return home, base, jnp.where(lent, 512 + step * GROUP, home * GROUP), row

    def fetch(block, slot):
        home, base, code_row, _ = place(block)
        x = home // 4
        yb = home % 4
        name = codes[pl.ds(pl.multiple_of(code_row, GROUP), GROUP), :]
        present = (name >= 0) & (block < own_blocks + lent_blocks)
        name = jnp.where(present, name, 0)
        side = name >> 9
        site = name & 511
        a = (side * 11) >> 5
        c = side - 3 * a
        ex = a * 8 + (site >> 6) - 6 - x
        ey = c * 8 + ((site >> 3) & 7) - 6 - 2 * yb
        local = ex * 48 + ey * 8 + (site & 7)
        local = jnp.where(present, local, -1)
        spread = nn(local.astype(F32).astype(BF16), slot_pick_ref[...])
        yield
        index = jnp.sum(spread * atom_mask_ref[...].astype(F32), axis=0, keepdims=True)
        hot[slot, 0:240, :] = jnp.where(hot_rows == index, 1.0, 0.0).astype(BF16)
        hot[slot, 240:256, :] = atom_mask_ref[...]
        yield
        parts = [far_tab[pl.ds(pl.multiple_of(base + 96 * i, 16), 48), :] for i in range(5)]
        parts.append(own_tab[pl.ds(pl.multiple_of(base + 208, 16), 16), :])
        table = jnp.concatenate(parts, axis=0)
        picked = tn(table, hot[slot])
        yield
        gat[slot] = picked

    def network(block, slot):
        mask = atom_mask_ref[...].astype(F32)
        wide_mask = atom_wide_ref[...].astype(F32)

        def prepare(k):
            species_row = lax.broadcasted_iota(jnp.int32, (8, PAIRS), 0).astype(F32)
            hot_own = jnp.where(species_row == feat[slot + k, 17:18, :], 1.0, 0.0)
            hot_far = jnp.where(species_row == feat[slot + k, 18:19, :], 1.0, 0.0)
            nil = jnp.zeros((8, PAIRS), F32)
            x0[k] = jnp.concatenate([feat[slot + k, 0:8, :], hot_own, hot_far, nil], axis=0).astype(BF16)
            for i in range(8):
                hbd[k, 16 * i : 16 * i + 16, :] = (feat[slot + k, 8 + i : 9 + i, :] * mask).astype(BF16)
            hbd[k, 128:144, :] = atom_mask_ref[...]
            yield

        def env(k, cols):
            return feat[slot + k, 16:17, cols]

        sums = {}

        def gather_sum(key, part):
            sums[key] = sums[key] + part if key in sums else part

        def stage_a(k, cols):
            half = nn(embed_t[:, 0:32], x0[k, :, cols])
            yield
            value, slope = swish(half)
            ss[k, 0, :, cols] = value.astype(BF16)
            dd[k, 0, :, cols] = (slope * (0.5 * env(k, cols))).astype(BF16)
            latent = value * env(k, cols)
            packed = latent.astype(BF16)
            j0[k, 0:128, cols] = packed
            we = nn(we_t[...], packed)
            yield
            w_s[k, :, cols] = we[0:32]
            coeff = we[32:64].astype(BF16)
            cat[k, 224:256, cols] = coeff
            gather_sum(("e0", k), nt(coeff, hbd[k, :, cols]))
            yield

        def between_a(k):
            environ = sums["e0", k] * NORM
            sums["e0", k] = environ
            eb[k, 0, :, 0:144] = (jnp.concatenate([environ] * 3, axis=0) * degree_mask_ref[...]).astype(BF16)
            e0t[k, :, 0:32] = environ.T.astype(BF16)
            yield
            spread = nn(e0t[k, :, 0:32], chan_wide_ref[...])
            yield
            for i in range(9):
                e0x[k, i : i + 1, :] = jnp.sum(
                    spread[16 * i : 16 * i + 16, :] * wide_mask, axis=0, keepdims=True
                )

        def stage_b(k, cols):
            q = nn(eb[k, 0, :, 0:144], hbd[k, :, cols])
            yield
            q_s[k, :, cols] = q
            w3 = jnp.concatenate([w_s[k, :, cols]] * 3, axis=0)
            scal = (q * w3).astype(BF16)
            j0[k, 128:224, cols] = scal
            half = nn(l1_t[:, 0:224], j0[k, :, cols])
            mixed = nn(mix_t[:, 0:32], scal[0:32])
            yield
            a_s[k, :, cols] = mixed
            value, slope = swish(half)
            ss[k, 1, :, cols] = value.astype(BF16)
            dd[k, 1, :, cols] = (slope * (0.5 * env(k, cols))).astype(BF16)
            latent = j0[k, 0:128, cols].astype(F32) + value * env(k, cols)
            packed = latent.astype(BF16)
            j1[k, 0:128, cols] = packed
            coeff = nn(e1_t[...], packed)
            yield
            coeff = coeff.astype(BF16)
            cat[k, 192:224, cols] = coeff
            gather_sum(("e1", k), nt(coeff, hbd[k, :, cols]))
            yield

        def spread_w(k, half):
            w = w_s[k, :, halves[half]]
            m8 = mask[8 * half : 8 * half + 8, halves[half]]
            return jnp.concatenate([w * m8[p : p + 1, :] for p in range(8)], axis=0).astype(BF16)

        def stage_c(k):
            environ = sums["e1", k] * NORM
            sums["e1", k] = environ
            eb[k, 1, :, 0:144] = (jnp.concatenate([environ] * 3, axis=0) * degree_mask_ref[...]).astype(BF16)
            e1r[k, :, 0:16] = jnp.concatenate(
                [environ[:, 16 * i : 16 * i + 16] for i in range(9)], axis=0
            ).astype(BF16)
            yield
            for i in range(9):
                e1x[k, 32 * i : 32 * i + 32, :] = nn(e1r[k, 32 * i : 32 * i + 32, 0:16], atom_wide_ref[...])
            for half in range(2):
                ww[k, half] = spread_w(k, half)
            yield
            for d in range(3):
                total = None
                for i in range(9):
                    if DEGREE_OF[i] == d:
                        part = e1x[k, 32 * i : 32 * i + 32, :] * e0x[k, i : i + 1, :]
                        total = part if total is None else total + part
                rows = slice(32 * d, 32 * d + 32)
                bmat[k, rows, :] = (total * mix_wide[rows, :]).astype(BF16)
            yield
            for half in range(2):
                r_s[k, :, halves[half]] = nn(bmat[k, :, wides[half]], ww[k, half])
            yield

        def stage_d(k, cols):
            q = nn(eb[k, 1, :, 0:144], hbd[k, :, cols])
            yield
            a = a_s[k, :, cols]
            q1_s[k, :, cols] = q
            j1[k, 128:224, cols] = (a * q + r_s[k, :, cols]).astype(BF16)
            half = nn(l2_t[:, 0:224], j1[k, :, cols])
            yield
            value, slope = swish(half)
            ss[k, 2, :, cols] = value.astype(BF16)
            dd[k, 2, :, cols] = (slope * (0.5 * env(k, cols))).astype(BF16)
            latent = j1[k, 0:128, cols].astype(F32) + value * env(k, cols)
            half = nn(out_t[...], latent.astype(BF16))
            yield
            hidden, slope = swish(half)
            weighted = eighth(hidden * vec_b[...])
            t_s[k, :, cols] = weighted
            dz = (slope * vec_b[...] * (0.5 * env(k, cols))).astype(BF16)
            dzs[k, 0:128, cols] = dz
            dl = nn(out_ref[...], dz)
            pair_energy[k, :, cols] = jnp.sum(weighted, axis=0, keepdims=True) * env(k, cols)
            yield
            t_s[k, :, cols] = t_s[k, :, cols] + eighth(dl * ss[k, 2, :, cols].astype(F32))
            dz = (dl * dd[k, 2, :, cols].astype(F32)).astype(BF16)
            dzs[k, 128:256, cols] = dz
            dscal = nn(latent_ref[1, 128:224, :], dz)
            yield
            ds_b[k, :, cols] = dscal.astype(BF16)
            dmix = nn(mix_all[:, 0:96], (dscal * q1_s[k, :, cols]).astype(BF16))
            dq = (dscal * a_s[k, :, cols]).astype(BF16)
            cat[k, 0:96, cols] = dq
            gather_sum(("d1", k), nt(dq, hbd[k, :, cols]))
            yield
            small[k, :, cols] = dmix

        def stage_e(k):
            row = pair_energy[k]
            high, middle, low = pieces(row, 3)
            fill = jnp.zeros((5, PAIRS), F32)
            total = nt(jnp.concatenate([high, middle, low, fill], axis=0).astype(BF16), atom_mask_ref[...])
            energy_ref[pl.ds(place(block + k)[3], 1), :] = total[0:1] + (total[1:2] + total[2:3])
            for half in range(2):
                db[k, :, wides[half]] = nt(ds_b[k, :, halves[half]], ww[k, half])
                back = tn(bmat[k, :, wides[half]], ds_b[k, :, halves[half]])
                m8 = mask[8 * half : 8 * half + 8, halves[half]]
                total = back[0:32] * m8[0:1]
                for p in range(1, 8):
                    total = total + back[32 * p : 32 * p + 32] * m8[p : p + 1]
                dwr[k, :, halves[half]] = total
            yield
            inner = []
            for i in range(9):
                rows = slice(32 * DEGREE_OF[i], 32 * DEGREE_OF[i] + 32)
                piece = db[k, rows, :] * mix_wide[rows, :]
                outer[k, 32 * i : 32 * i + 32, :] = (piece * e0x[k, i : i + 1, :]).astype(BF16)
                inner.append(jnp.sum(piece * e1x[k, 32 * i : 32 * i + 32, :], axis=0, keepdims=True))
            yield
            side = nt(outer[k], atom_wide_ref[...])
            de0t = nt(jnp.concatenate([r * wide_mask for r in inner], axis=0).astype(BF16), chan_wide_ref[...])
            yield
            de = sums["d1", k] * degree_mask_ref[...]
            de = de[0:32] + de[32:64] + de[64:96]
            de = de + jnp.concatenate([side[32 * i : 32 * i + 32, :] for i in range(9)], axis=1)
            de = de * NORM
            sums["d1", k] = de
            de_b[k, 1, :, 0:144] = de.astype(BF16)
            sums["side0", k] = de0t.T

        def stage_f(k, cols):
            dcoeff = nn(de_b[k, 1, :, 0:144], hbd[k, :, cols])
            yield
            dzs[k, 256:288, cols] = dcoeff.astype(BF16)
            dl = nn(back_w[:, 0:288], dzs[k, 0:288, cols])
            yield
            t_s[k, :, cols] = t_s[k, :, cols] + eighth(dl * ss[k, 1, :, cols].astype(F32))
            dz = (dl * dd[k, 1, :, cols].astype(F32)).astype(BF16)
            dzs[k, 288:416, cols] = dz
            dscal = nn(latent_ref[0, 128:224, :], dz)
            yield
            dscal = [dscal[0:32] + small[k, :, cols], dscal[32:64], dscal[64:96]]
            w = w_s[k, :, cols]
            dw = dwr[k, :, cols]
            for d in range(3):
                cat[k, 96 + 32 * d : 128 + 32 * d, cols] = (dscal[d] * w).astype(BF16)
                dw = dw + dscal[d] * q_s[k, 32 * d : 32 * d + 32, cols]
            dzs[k, 416:448, cols] = dw.astype(BF16)
            gather_sum(("d0", k), nt(cat[k, 96:192, cols], hbd[k, :, cols]))
            yield

        def between_f(k):
            de = sums["d0", k] * degree_mask_ref[...]
            de = (de[0:32] + de[32:64] + de[64:96] + sums["side0", k]) * NORM
            de_b[k, 0, :, 0:144] = de.astype(BF16)
            yield
            e0, e1, d1 = sums["e0", k], sums["e1", k], sums["d1", k]
            tall = []
            for e in (e1, e0):
                three = jnp.concatenate([e[:, 0:128]] * 3, axis=0)
                tall.append(three * degree_mask_ref[:, 0:128])
            tall += [d1[:, 0:128], de[:, 0:128]]
            left[k] = jnp.concatenate(tall, axis=0).T.astype(BF16)
            yield

        def stage_h(k, cols):
            dcoeff = nn(de_b[k, 0, :, 0:144], hbd[k, :, cols])
            dhbd = nn(left[k], cat[k, :, cols])
            yield
            dzs[k, 448:480, cols] = dcoeff.astype(BF16)
            dl = nn(back_w[:, 0:480], dzs[k, 0:480, cols])
            for i in range(8):
                dfeat[slot + k, 8 + i : 9 + i, cols] = jnp.sum(
                    dhbd[16 * i : 16 * i + 16, :] * mask[:, cols], axis=0, keepdims=True
                )
            yield
            dz = (dl * dd[k, 0, :, cols].astype(F32)).astype(BF16)
            dradial = nn(embed_ref[...], dz)
            dfeat[slot + k, 16:17, cols] = jnp.sum(
                t_s[k, :, cols] + eighth(dl * ss[k, 0, :, cols].astype(F32)), axis=0, keepdims=True
            )
            yield
            dfeat[slot + k, 0:8, cols] = dradial[0:8]

        members = range(UNIT)
        for stage, tiled in (
            (prepare, False),
            (stage_a, True),
            (between_a, False),
            (stage_b, True),
            (stage_c, False),
            (stage_d, True),
            (stage_e, False),
            (stage_f, True),
            (between_f, False),
            (stage_h, True),
        ):
            if tiled:
                together([stage(k, cols) for k in members for cols in tiles])
            else:
                together([stage(k) for k in members])

    def scatter(block, slot):
        pulled = nt(hot[slot], dfeat[slot, 0:16, :].astype(BF16))
        yield
        _, base, _, _ = place(block)
        for i in range(5):
            rows = pl.ds(pl.multiple_of(base + 96 * i, 16), 48)
            ftab[rows, :] = ftab[rows, :] - pulled[48 * i : 48 * i + 48, :]
        rows = pl.ds(pl.multiple_of(base + 208, 16), 16)
        ftab[rows, :] = ftab[rows, :] + pulled[240:256, :]

    blocks = own_blocks + lent_blocks

    def chunk_step(chunk, carry):
        first = chunk * CHUNK

        def rows_of(ref):
            return lambda f: jnp.concatenate([ref[b, f : f + 1, :] for b in range(CHUNK)], axis=0)

        def rows_to(ref):
            def put(f, value):
                for b in range(CHUNK):
                    ref[b, f : f + 1, :] = value[b : b + 1, :]

            return put

        together([fetch(first + k, k) for k in range(UNIT)])
        geometry(rows_of(gat), rows_to(feat), geo)
        network(first, 0)
        geometry_back(rows_of(dfeat), rows_to(dfeat), geo)
        together([scatter(first + k, k) for k in range(UNIT)])
        return carry

    lax.fori_loop(0, (blocks + CHUNK - 1) // CHUNK, chunk_step, 0)

    def leave(force_ref, per_plane, first_y, planes=12, first_row=0):
        rows = jnp.concatenate(
            [
                ftab[first_row + p * 96 + first_y * LZ : first_row + p * 96 + first_y * LZ + per_plane, :]
                for p in range(planes)
            ],
            axis=0,
        )
        turned_rows = rows.T
        force_ref[...] = turned_rows[0:3] + turned_rows[3:6]

    leave(fmid_ref, 64, 2)
    leave(flow_ref, 16, 0)
    leave(fhigh_ref, 16, 10)
    leave(flent_ref, 96, 0, 6, 1152)


def pair_call(blocks, mid, low, high, neighbors, used, lent, lent_sites, params):
    embed, first, env, latent, mix, out, vector = params
    sites = neighbors.shape[0]
    atom_mask, slot_pick, atom_wide, chan_wide, degree_mask = constants()
    consts = [
        jnp.asarray(atom_mask, BF16),
        jnp.asarray(slot_pick, BF16),
        jnp.asarray(atom_wide, BF16),
        jnp.asarray(chan_wide, BF16),
        jnp.asarray(degree_mask, F32),
    ]
    vm = pl.BlockSpec(memory_space=pltpu.VMEM)
    sm = pl.BlockSpec(memory_space=pltpu.SMEM)
    scratch = [
        ((608, SLOTS), jnp.int32),
        ((1728, 16), BF16),
        ((1728, 16), BF16),
        ((1728, 16), F32),
        ((128, 128), BF16),
        ((64, 128), BF16),
        ((128, 256), BF16),
        ((128, 256), BF16),
        ((32, 128), BF16),
        ((128, 128), BF16),
        ((96, 128), BF16),
        ((32, 128), BF16),
        ((96, 512), F32),
        ((128, TILE), F32),
        ((CHUNK, 256, PAIRS), BF16),
        ((CHUNK, 16, PAIRS), F32),
        ((CHUNK, 24, PAIRS), F32),
        ((CHUNK, 24, PAIRS), F32),
        ((14, CHUNK, PAIRS), F32),
        ((UNIT, 32, PAIRS), BF16),
        ((UNIT, 144, PAIRS), BF16),
        ((UNIT, 3, 128, PAIRS), BF16),
        ((UNIT, 3, 128, PAIRS), BF16),
        ((UNIT, 224, PAIRS), BF16),
        ((UNIT, 224, PAIRS), BF16),
        ((UNIT, 32, PAIRS), F32),
        ((UNIT, 256, PAIRS), BF16),
        ((UNIT, 96, PAIRS), F32),
        ((UNIT, 96, PAIRS), F32),
        ((UNIT, 96, PAIRS), F32),
        ((UNIT, 96, PAIRS), F32),
        ((UNIT, 96, PAIRS), BF16),
        ((UNIT, 8, PAIRS), F32),
        ((UNIT, 32, PAIRS), F32),
        ((UNIT, 32, PAIRS), F32),
        ((UNIT, 16, 512), F32),
        ((UNIT, 288, 512), F32),
        ((UNIT, 96, 512), BF16),
        ((UNIT, 2, 96, 256), BF16),
        ((UNIT, 144, 128), BF16),
        ((UNIT, 288, 128), BF16),
        ((UNIT, 2, 256, 384), BF16),
        ((UNIT, 1, PAIRS), F32),
        ((UNIT, 96, 512), F32),
        ((UNIT, 288, 512), BF16),
        ((UNIT, 2, 32, 256), BF16),
        ((UNIT, 128, 256), BF16),
        ((UNIT, 480, PAIRS), BF16),
        ((128, 512), BF16),
    ]
    return pl.pallas_call(
        pair_kernel,
        out_shape=[
            jax.ShapeDtypeStruct((sites // GROUP + 8, GROUP), F32),
            jax.ShapeDtypeStruct((3, 768), F32),
            jax.ShapeDtypeStruct((3, 192), F32),
            jax.ShapeDtypeStruct((3, 192), F32),
            jax.ShapeDtypeStruct((3, 576), F32),
        ],
        in_specs=[sm] + [vm] * 19,
        out_specs=[vm] * 5,
        scratch_shapes=[pltpu.VMEM(shape, dtype) for shape, dtype in scratch],
        compiler_params=pltpu.CompilerParams(vmem_limit_bytes=48 * 1024 * 1024),
        name="pair_terms",
    )(blocks, mid, low, high, neighbors, used, lent, lent_sites, embed, first, env, latent, mix[0], out, vector.reshape(1, -1), *consts)


def route_kernel(me_ref, shares_ref, boxes_ref, forward_ref, lender_ref, blocks_ref):
    count = shares_ref.shape[0]
    me = me_ref[0]
    down = lax.broadcasted_iota(jnp.int32, (count, count), 0)
    right = lax.broadcasted_iota(jnp.int32, (count, count), 1)
    need = shares_ref[:, 3 * SHARE : 3 * SHARE + 1]
    need_down = jnp.broadcast_to(need, (count, count))
    need_right = jnp.sum(jnp.where(down == right, need_down, 0.0), axis=0, keepdims=True)
    need_right = jnp.broadcast_to(need_right, (count, count))
    full_down = need_down > LIGHT_BLOCKS + 0.5
    full_right = need_right > LIGHT_BLOCKS + 0.5
    rank_down = jnp.sum(jnp.where(full_right & (right < down), 1.0, 0.0), axis=1, keepdims=True)
    rank_down = jnp.broadcast_to(rank_down, (count, count))
    rank_right = jnp.sum(jnp.where(full_down & (down < right), 1.0, 0.0), axis=0, keepdims=True)
    rank_right = jnp.broadcast_to(rank_right, (count, count))
    light_down = jnp.where(full_down, -1.0, down.astype(F32) - rank_down)
    light_right = jnp.where(full_right, -1.0, right.astype(F32) - rank_right)
    lends_right = jnp.where(full_right, 3.0 * rank_right, 1000.0)
    lends_down = jnp.where(full_down, 3.0 * rank_down, 1000.0)
    total = jnp.zeros((count, SHARE), F32)
    boxes = jnp.zeros((count, BOX), F32)
    lender = jnp.zeros((count, 1), F32)
    parts = jnp.zeros((count, 1), F32)
    for j in range(3):
        choice = jnp.where(light_down == lends_right + j, 1.0, 0.0)
        names = shares_ref[:, j * SHARE : (j + 1) * SHARE]
        high, low = pieces(names, 2)
        choice_b = choice.astype(BF16)
        total = total + (nn(choice_b, high.astype(BF16)) + nn(choice_b, low.astype(BF16)))
        mine = jnp.sum(jnp.where(right == me, choice, 0.0), axis=1, keepdims=True)
        boxes = boxes + mine * boxes_ref[j : j + 1, :]
        taken = jnp.where((light_right == lends_down + j) & (right == me), 1.0, 0.0)
        taken = jnp.sum(taken, axis=1, keepdims=True)
        lender = lender + taken
        parts = parts + j * taken
    forward_ref[:, 0:SHARE] = total
    forward_ref[:, SHARE : SHARE + BOX] = boxes
    lender_ref[...] = lender
    here = lax.broadcasted_iota(jnp.int32, (count, 1), 0) == me
    own_need = jnp.sum(jnp.where(here, need, 0.0)).astype(jnp.int32)
    lent_need = jnp.sum(lender * need).astype(jnp.int32)
    part = jnp.sum(parts).astype(jnp.int32)
    first = KEPT + LENT * part
    blocks_ref[0] = jnp.where(own_need > LIGHT_BLOCKS, jnp.minimum(own_need, KEPT), own_need)
    blocks_ref[1] = jnp.minimum(jnp.maximum(lent_need - first, 0), LENT)
    blocks_ref[2] = first
    blocks_ref[3] = part


def route_call(me, shares, boxes):
    count = shares.shape[0]
    vm = pl.BlockSpec(memory_space=pltpu.VMEM)
    sm = pl.BlockSpec(memory_space=pltpu.SMEM)
    return pl.pallas_call(
        route_kernel,
        out_shape=[
            jax.ShapeDtypeStruct((count, SHARE + BOX), F32),
            jax.ShapeDtypeStruct((count, 1), F32),
            jax.ShapeDtypeStruct((4,), jnp.int32),
        ],
        in_specs=[sm, vm, vm],
        out_specs=[vm, vm, sm],
        name="route",
    )(me, shares, boxes)


def ring(axis, by):
    count = lax.axis_size(axis)
    return [(i, (i + by) % count) for i in range(count)]


def on_device(positions, species, neighbors, slot_used, *params):
    sites = species.shape[-1]
    count = lax.axis_size("yz")
    me = lax.axis_index("yz")
    near = neighbors.reshape(sites, SLOTS)
    used = slot_used.reshape(sites, SLOTS)
    own = jnp.concatenate(
        [positions.reshape(3, sites), species.reshape(1, sites).astype(F32)], axis=0
    )
    up_x, down_x = ring("gx", 1), ring("gx", -1)
    before = lax.ppermute(own[:, 384:512], "gx", up_x)
    after = lax.ppermute(own[:, 0:128], "gx", down_x)
    mid = jnp.concatenate([before, own, after], axis=1)
    planes = mid.reshape(4, 12, 64)
    filled = jnp.max(jnp.where(used > 0, lax.broadcasted_iota(jnp.int32, used.shape, 0) + 1, 0))
    need = (filled + GROUP - 1) // GROUP

    last = slice(KEPT * GROUP, sites)
    codes = jnp.where(used[last] > 0, near[last], -1).astype(F32).reshape(3, count, SHARE)
    shares = codes.transpose(1, 0, 2).reshape(count, 3 * SHARE)
    device = jnp.arange(count, dtype=jnp.int32)
    me_low = (device == (me + count - 1) % count).astype(F32)[:, None]
    me_high = (device == (me + 1) % count).astype(F32)[:, None]
    shares = jnp.concatenate(
        [
            shares,
            jnp.full((count, 1), need, jnp.int32).astype(F32),
            me_high * planes[:, :, 48:64].reshape(1, 768),
            me_low * planes[:, :, 0:16].reshape(1, 768),
        ],
        axis=1,
    )
    shares = lax.all_to_all(shares, "yz", 0, 0, tiled=True)
    edges = jnp.sum(shares[:, 3 * SHARE + 1 :], axis=0)
    low = edges[0:768].reshape(4, 192)
    high = edges[768:1536].reshape(4, 192)
    box = jnp.concatenate([low.reshape(4, 12, 16), planes, high.reshape(4, 12, 16)], axis=2)
    firsts = [KEPT + LENT * j for j in range(3)]
    boxes = jnp.concatenate([box[:, f // 4 : f // 4 + 6].reshape(1, BOX) for f in firsts], axis=0)
    forward, lender, blocks = route_call(me.astype(jnp.int32).reshape(1), shares, boxes)
    lent = lax.all_to_all(forward, "yz", 0, 0, tiled=True)
    lent_codes = lent[:, 0:SHARE].reshape(2 * SLOTS, SLOTS)
    lent_sites = jnp.sum(lent[:, SHARE:] * lender, axis=0).reshape(4, 576)
    part = blocks[3]

    energy, fmid, flow, fhigh, flent = pair_call(
        blocks, mid, low, high, near, used, lent_codes, lent_sites, params
    )

    lent_force = flent.reshape(3, 6, 96)
    wide = sum(
        jnp.where(part == j, jnp.pad(lent_force, ((0, 0), (f // 4, 6 - f // 4), (0, 0))), 0.0)
        for j, f in enumerate(firsts)
    )

    def to_low(edge):
        return jnp.pad(edge, ((0, 0), (0, 0), (48, 0))).reshape(1, -1)

    def to_high(edge):
        return jnp.pad(edge, ((0, 0), (0, 0), (0, 48))).reshape(1, -1)

    home = lender
    home_low = jnp.roll(lender, -1, axis=0)
    home_high = jnp.roll(lender, 1, axis=0)
    sent = (
        home * wide[:, :, 16:80].reshape(1, -1)
        + home_low * to_low(wide[:, :, 0:16])
        + home_high * to_high(wide[:, :, 80:96])
        + me_low * to_low(flow.reshape(3, 12, 16))
        + me_high * to_high(fhigh.reshape(3, 12, 16))
    )
    lent_energy = energy[32:38].reshape(1, 96)
    parts = [jnp.where(part == j, home * lent_energy, 0.0) for j in range(3)]
    got = lax.all_to_all(jnp.concatenate([sent] + parts, axis=1), "yz", 0, 0, tiled=True)
    got = jnp.sum(got, axis=0)
    column = fmid + got[0:2304].reshape(3, 768)
    own_energy = energy[0:32].reshape(sites) + jnp.pad(got[2304:2592], (KEPT * GROUP, 0))
    from_after = lax.ppermute(column[:, 0:128], "gx", down_x)
    from_before = lax.ppermute(column[:, 640:768], "gx", up_x)
    gap = jnp.zeros((3, 256), F32)
    forces = column[:, 128:640] + jnp.concatenate([from_before, gap, from_after], axis=1)
    return (own_energy.reshape(1, 1, sites), forces.reshape(3, 1, 1, sites))


def solution(mesh):
    in_specs = (
        P(None, "gx", "yz", None),
        P("gx", "yz", None),
        P("gx", "yz", None, None),
        P("gx", "yz", None, None),
        P(),
        P(),
        P(),
        P(),
        P(),
        P(),
        P(),
    )
    out_specs = (P("gx", "yz", None), P(None, "gx", "yz", None))
    return jax.shard_map(
        on_device, mesh=mesh, in_specs=in_specs, out_specs=out_specs, check_vma=False
    )
```
